256 devices in a mesh: row: 32 (over z, x), col: 8 (over y, core).
Axes of the slice: x: 4, y: 4, z: 8, core: 2. Of those that a mesh axis runs over, the one named last changes fastest.
Arguments:
- right_sides: bfloat16 [4, 512, 32, 256], P(None, 'row', 'col'), may hold values from -6 to 6
- lower_blocks: bfloat16 [6, 32, 32, 256, 256], P(None, 'col', 'row'), may hold values from -0.21875 to 0.21875
- lower_fill: int32 [6, 32, 32], P(None, 'col', 'row'), may hold values from 0 to 1, as said below
- upper_blocks: bfloat16 [6, 32, 32, 256, 256], P(None, 'col', 'row'), may hold values from -0.21875 to 0.21875
- upper_fill: int32 [6, 32, 32], P(None, 'col', 'row'), may hold values from 0 to 1, as said below
- lower_inv: bfloat16 [4, 32, 256, 256], P(None, 'col')
- upper_inv: bfloat16 [4, 32, 256, 256], P(None, 'col')
Outputs:
- solution: float32 [4, 512, 32, 256], P(None, 'row', 'col')
The draws below stay inside these ranges and needn't reach their ends.
Inputs may be any that keep to these rules, and one draw needn't show every extreme that they name: The fill follows an elimination forest: each supernode of a level below the top has one parent on the next level; lower_fill at [a (a - 1) / 2 + b, i, j] is 1 exactly when supernode i of level a is the ancestor of supernode j of level b, else 0. The same forest as lower_fill with the two supernode indices swapped: upper_fill at [a (a - 1) / 2 + b, i, j] is 1 exactly when supernode j of level a is the ancestor of supernode i of level b.
All inputs are finite; a program needn't handle non-finite values.
Results may differ from the reference program's by a relative error of at most 0.007.
Values may be sent and summed in bfloat16 or wider, within the bound.
A program may use at most 64 MiB of HBM per device.

```python
import jax
import jax.numpy as jnp
from jax import lax

W = 256
NRHS = 512
LEV = 4
NS = 32
PAIRS = 6


def assemble(diagonal, off_diagonal):
    identity = (jnp.arange(W)[:, None] == jnp.arange(W)[None, :]).astype(jnp.float32)
    return identity * diagonal + off_diagonal


def forest_fill(key):
    parents = jax.random.randint(key, (LEV - 1, NS), 0, NS)
    columns = jnp.arange(NS)
    layers = []
    for upper_level in range(1, LEV):
        for lower_level in range(upper_level):
            ancestor = columns
            for step_level in range(lower_level, upper_level):
                ancestor = jnp.take(parents[step_level], ancestor)
            layers.append((columns[:, None] == ancestor[None, :]).astype(jnp.int32))
    return jnp.stack(layers)


def draw_lower_fill(key, part):
    return forest_fill(key)


def draw_upper_fill(key, part):
    return jnp.transpose(forest_fill(key), (0, 2, 1))


def draw_lower_inv(key, part):
    key = jax.random.fold_in(key, 11)
    diag_key, rough_key = jax.random.split(key)
    diagonal = jax.random.uniform(diag_key, (LEV, NS, 1, W), jnp.float32, 0.7, 1.3)
    off_diagonal = 0.4 * jnp.clip(jax.random.normal(rough_key, (LEV, NS, W, W), jnp.float32), -3.0, 3.0) / jnp.sqrt(1.0 * W)
    return assemble(diagonal, off_diagonal).astype(jnp.bfloat16)


def draw_upper_inv(key, part):
    key = jax.random.fold_in(key, 23)
    diag_key, rough_key = jax.random.split(key)
    diagonal = jax.random.uniform(diag_key, (LEV, NS, 1, W), jnp.float32, 0.7, 1.3)
    off_diagonal = 0.4 * jnp.clip(jax.random.normal(rough_key, (LEV, NS, W, W), jnp.float32), -3.0, 3.0) / jnp.sqrt(1.0 * W)
    return assemble(diagonal, off_diagonal).astype(jnp.bfloat16)


def steps_of(stream_key, dims, cuts, low, top_value):
    loudness = 1.0
    for position, parts in cuts:
        draws = jax.random.uniform(jax.random.fold_in(jax.random.fold_in(stream_key, 6), position), (parts,), jnp.float32, low / len(cuts), top_value / len(cuts))
        loudness = loudness * jnp.repeat(jnp.exp(draws), dims[position] // parts).reshape((-1,) + (1,) * (len(dims) - 1 - position))
    return loudness


def scatter_about(own_key, shape, width, most, pieces=(), kind=jnp.bfloat16):
    result = width * jax.random.normal(own_key, shape, jnp.float32)
    if pieces:
        result = result * steps_of(own_key, shape, pieces, -0.22, 0.18)
    return jnp.clip(result, -most, most).astype(kind)


def setup_inputs(seed: int = 0) -> dict:
    seeds = jax.random.split(jax.random.key(seed), 8)
    return {
        "right_sides": scatter_about(seeds[0], (LEV, NRHS, NS, W), 1.0, 6.0, ((1, 32), (2, 8))),
        "lower_blocks": scatter_about(seeds[1], (PAIRS, NS, NS, W, W), (3 * W) ** -0.5, 0.21875, ((1, 8), (2, 32))),
        "lower_fill": draw_lower_fill(jax.random.fold_in(seeds[7], 71), 0),
        "upper_blocks": scatter_about(seeds[3], (PAIRS, NS, NS, W, W), (3 * W) ** -0.5, 0.21875, ((1, 8), (2, 32))),
        "upper_fill": draw_upper_fill(jax.random.fold_in(seeds[7], 71), 0),
        "lower_inv": draw_lower_inv(jax.random.fold_in(seeds[7], 71), 0),
        "upper_inv": draw_upper_inv(jax.random.fold_in(seeds[7], 71), 0),
    }


def pair_index(current, earlier):
    upper_level = max(current, earlier)
    lower_level = min(current, earlier)
    return upper_level * (upper_level - 1) // 2 + lower_level


def level_sum(solution_rows, target_blocks, fill_masks):
    flattened = solution_rows.reshape(NRHS, NS * W)

    def one_target(packed):
        tiles, fill_row = packed
        masked = tiles * fill_row[:, None, None].astype(tiles.dtype)
        return jnp.dot(flattened, masked.reshape(NS * W, W), preferred_element_type=jnp.float32)

    per_target = lax.map(one_target, (target_blocks, fill_masks))
    return jnp.transpose(per_target, (1, 0, 2))


def triangular_sweep(right_sides, blocks, fills, inverses, level_order):
    solved = [None] * LEV
    rounded = [None] * LEV
    finished = []
    for current in level_order:
        running = jnp.zeros((NRHS, NS, W), jnp.float32)
        for earlier in finished:
            which = pair_index(current, earlier)
            running = running + level_sum(rounded[earlier], blocks[which], fills[which])
        residual = (right_sides[current].astype(jnp.float32) - running).astype(jnp.bfloat16)
        solved_block = jnp.einsum("rtv,tvw->rtw", residual.astype(jnp.float32), inverses[current].astype(jnp.float32))
        solved[current] = solved_block
        rounded[current] = solved_block.astype(jnp.bfloat16)
        finished.append(current)
    return solved, rounded


def reference(right_sides, lower_blocks, lower_fill, upper_blocks, upper_fill, lower_inv, upper_inv):
    ignored, forward = triangular_sweep(right_sides, lower_blocks, lower_fill, lower_inv, list(range(LEV)))
    middle = jnp.stack(forward)
    solution, unused = triangular_sweep(middle, upper_blocks, upper_fill, upper_inv, list(range(LEV - 1, -1, -1)))
    return jnp.stack(solution)
```

```python
import functools

import jax
import jax.numpy as jnp
from jax import lax
from jax.experimental import pallas as pl
from jax.experimental.pallas import tpu as pltpu
from jax.sharding import PartitionSpec as P

MESH = pl.DeviceIdType.MESH
F32 = jnp.float32
BF16 = jnp.bfloat16


def pair_index(current, earlier):
    upper_level = max(current, earlier)
    lower_level = min(current, earlier)
    return upper_level * (upper_level - 1) // 2 + lower_level


def sweep_kernel(
    dims, rhs, lower, lower_fill, upper, upper_fill, lower_inv, upper_inv, out,
    l_raw, u_raw, linv, uinv, l_loc, l_in, l_sum, l_home, u_in, u_sum, u_slice, u_home,
    rhs_home, fwd, flag_out, flag_x, flag_row, flag_all, flags,
    near, part_out, part_in, solved, pick_out, pick_in, pick_own, answer,
    load_sem, inv_sem, flag_sem,
    rhs_s, rhs_r, fx_s, fx_r, fd_s, fd_r, ly_s, ly_r, ld_s, ld_r, ux_s, ux_r, uz_s, uz_r,
    ua_s, ua_r, na_s, na_r, pb_s, pb_r, xa_s, xa_r, xb_s, xb_r, out_s, out_r,
):
    lev, nx, nc, rows, width = dims
    pairs = lev * (lev - 1) // 2
    nz = nc
    step = width // nc
    row = lax.axis_index("row")
    c = lax.axis_index("col")
    z = lax.div(row, nx)
    x = lax.rem(row, nx)
    diagonal = c == z

    def wrap(value, count):
        return lax.rem(value, count)

    def send(src, dst, ssem, rsem, to_row, to_col):
        pltpu.make_async_remote_copy(
            src_ref=src, dst_ref=dst, send_sem=ssem, recv_sem=rsem,
            device_id=(to_row, to_col), device_id_type=MESH,
        ).start()

    def wait(ref, sem):
        pltpu.make_async_copy(ref, ref, sem).wait()

    def x_peer(k):
        return z * nx + wrap(x + k, nx)

    def z_peer(k):
        return wrap(z + k, nz) * nx + x

    def each(count, body):
        def run(k, carry):
            body(k)
            return carry

        lax.fori_loop(1, count, run, 0)

    order = []
    for a in range(1, lev):
        for b in range(a):
            order.append(pair_index(a, b))
    back = []
    for b in range(lev - 2, -1, -1):
        for a in range(b + 1, lev):
            back.append(pair_index(a, b))

    def load_lower(p):
        return pltpu.make_async_copy(lower.at[p, :, 0], l_raw.at[p], load_sem.at[p])

    def load_upper(p):
        return pltpu.make_async_copy(upper.at[p, :, 0], u_raw.at[p], load_sem.at[pairs + p])

    def load_linv(l):
        return pltpu.make_async_copy(lower_inv.at[l, x], linv.at[l], inv_sem.at[l])

    def load_uinv(l):
        return pltpu.make_async_copy(upper_inv.at[l, x], uinv.at[l], inv_sem.at[lev + l])

    load_lower(order[0]).start()
    load_linv(0).start()
    for p in order[1:]:
        load_lower(p).start()
    for l in range(1, lev):
        load_linv(l).start()
    for p in back:
        load_upper(p).start()
    for l in range(lev - 1, -1, -1):
        load_uinv(l).start()

    barrier = pltpu.get_barrier_semaphore()

    def greet(to_row, to_col):
        pl.semaphore_signal(barrier, inc=1, device_id=(to_row, to_col), device_id_type=MESH)

    each(nx, lambda k: greet(x_peer(k), c))
    each(nc, lambda k: greet(row, wrap(c + k, nc)))
    each(nz, lambda k: greet(z_peer(k), c))

    def greet_diagonal(cc):
        @pl.when(jnp.logical_not(jnp.logical_and(diagonal, cc == c)))
        def _():
            greet(c * nx + x, cc)

    def greet_run(k, carry):
        greet_diagonal(k)
        return carry

    lax.fori_loop(0, nc, greet_run, 0)

    lane = lax.broadcasted_iota(jnp.int32, (8, 128), 1)
    for t in range(nx):
        tile = jnp.zeros((8, 128), F32)
        for p in range(pairs):
            tile = jnp.where(lane == p, lower_fill[p, t, 0].astype(F32), tile)
            tile = jnp.where(lane == pairs + p, upper_fill[p, t, 0].astype(F32), tile)
        flag_out[t] = tile
    flag_x[x] = flag_out[x]

    pl.semaphore_wait(barrier, (nx - 1) + (nc - 1) + (nz - 1) + nc - diagonal.astype(jnp.int32))

    own_rows = pl.ds(pl.multiple_of(x * rows, rows), rows)

    def start_x(k):
        target = wrap(x + k, nx)
        send(flag_out.at[target], flag_x.at[x], fx_s, fx_r, x_peer(k), c)
        send(rhs.at[target], rhs_home.at[:, own_rows, :], rhs_s, rhs_r, x_peer(k), c)

    each(nx, start_x)
    pltpu.make_async_copy(rhs.at[x], rhs_home.at[:, own_rows, :], rhs_r).start()

    def chunk(index):
        return pl.ds(pl.multiple_of(index * step, step), step)

    def lower_to_columns(p):
        load_lower(p).wait()
        found = jnp.zeros((width, width), BF16)
        for t in range(nx):
            found = lax.select(lower_fill[p, t, 0] != 0, l_raw[p, t], found)
        l_loc[p] = found

        def go(k):
            peer = wrap(c + k, nc)
            send(l_loc.at[p, chunk(peer)], l_in.at[p, k - 1], ly_s.at[p], ly_r.at[p], row, peer)

        each(nc, go)

    def over_z(body):
        def run(zz, carry):
            same = jnp.logical_and(zz == z, diagonal)

            @pl.when(same)
            def _():
                body(zz, True)

            @pl.when(jnp.logical_not(same))
            def _():
                body(zz, False)

            return carry

        lax.fori_loop(0, nz, run, 0)

    def lower_to_home(p):
        wait(l_in.at[p], ly_r.at[p])
        total = l_loc[p, chunk(c), :]
        for k in range(nc - 1):
            total = total + l_in[p, k]
        l_sum[p] = total

        def go(zz, same):
            if same:
                pltpu.make_async_copy(l_sum.at[p], l_home.at[p, chunk(c)], ld_r.at[p]).start()
            else:
                send(
                    l_sum.at[p], l_home.at[p, chunk(c)], ld_s.at[p], ld_r.at[p],
                    zz * nx + x, z,
                )

        over_z(go)

    def flags_to_home():
        wait(flag_x.at[pl.ds(0, nx - 1)], fx_r)
        sub = lax.broadcasted_iota(jnp.int32, (8, 128), 0)
        tile = jnp.zeros((8, 128), F32)
        for k in range(nx):
            tile = jnp.where(sub == k, flag_x[k], tile)
        flag_row[...] = tile

        def go(zz, same):
            if same:
                pltpu.make_async_copy(flag_row, flag_all.at[c], fd_r).start()
            else:
                send(flag_row, flag_all.at[c], fd_s, fd_r, zz * nx + x, z)

        over_z(go)

    def flags_ready():
        wait(flag_all, fd_r)
        copy = pltpu.make_async_copy(flag_all, flags, flag_sem)
        copy.start()
        copy.wait()

    def upper_over_x(p):
        load_upper(p).wait()
        for t in range(nx):
            u_raw[p, t] = lax.select(
                upper_fill[p, t, 0] != 0, u_raw[p, t], jnp.zeros((width, width), BF16)
            )

        def go(k):
            send(u_raw.at[p, wrap(x + k, nx)], u_in.at[p, k - 1], ux_s.at[p], ux_r.at[p], x_peer(k), c)

        each(nx, go)

    def upper_over_z(p):
        wait(u_in.at[p], ux_r.at[p])
        total = u_raw[p, x]
        for k in range(nx - 1):
            total = total + u_in[p, k]
        u_sum[p] = total

        def go(k):
            send(
                u_sum.at[p, chunk(wrap(z + k, nz))], u_slice.at[p, k - 1], uz_s.at[p], uz_r.at[p],
                z_peer(k), c,
            )

        each(nz, go)

    def upper_to_all(p):
        wait(u_slice.at[p], uz_r.at[p])
        total = u_sum[p, chunk(z), :]
        for k in range(nz - 1):
            total = total + u_slice[p, k]
        u_home[p, chunk(z), :] = total

        def go(k):
            send(u_home.at[p, chunk(z)], u_home.at[p, chunk(z)], ua_s.at[p], ua_r.at[p], z_peer(k), c)

        each(nz, go)

    def product(left, right):
        return jnp.dot(left, right, preferred_element_type=F32)

    def contribute(a, b):
        p = pair_index(a, b)
        wait(l_home.at[p], ld_r.at[p])
        near[p, x] = product(fwd[b], l_home[p]).astype(BF16)
        each(nx, lambda k: send(near.at[p, x], near.at[p, x], na_s.at[p], na_r.at[p], x_peer(k), c))

    def mix(column, level):
        total = None
        for m in range(level):
            p = pair_index(level, m)
            for k in range(nx):
                term = near[p, k].astype(F32) * flags[column, k, p]
                total = term if total is None else total + term
        return total

    def spread_parts(level):
        for m in range(level):
            p = pair_index(level, m)
            wait(near.at[p, pl.ds(0, nx - 1)], na_r.at[p])

        def go(k):
            peer = wrap(c + k, nc)
            part_out[level - 1, k - 1] = mix(peer, level).astype(BF16)
            send(
                part_out.at[level - 1, k - 1], part_in.at[level - 1, k - 1],
                pb_s.at[level - 1], pb_r.at[level - 1], row, peer,
            )

        each(nc, go)

    def collect_parts(level):
        total = mix(c, level)
        wait(part_in.at[level - 1], pb_r.at[level - 1])
        for k in range(nc - 1):
            total = total + part_in[level - 1, k].astype(F32)
        return (rhs_home[level].astype(F32) - total).astype(BF16)

    def solve_lower(level, residual):
        load_linv(level).wait()
        fwd[level] = product(residual, linv[level]).astype(BF16)

    def solve_upper(level, residual):
        load_uinv(level).wait()
        result = product(residual, uinv[level])
        if level:
            solved[level, x] = result.astype(BF16)
            each(
                nx,
                lambda k: send(
                    solved.at[level, x], solved.at[level, x], xa_s.at[level], xa_r.at[level],
                    x_peer(k), c,
                ),
            )
        answer[level] = result

        def go(k):
            target = wrap(x + k, nx)
            there = pl.ds(pl.multiple_of(target * rows, rows), rows)
            send(answer.at[level, there], out.at[level, x], out_s.at[level], out_r.at[level], x_peer(k), c)

        each(nx, go)
        pltpu.make_async_copy(answer.at[level, own_rows], out.at[level, x], out_r.at[level]).start()

    def choose(column, a, p):
        total = None
        for k in range(nx):
            term = solved[a, k].astype(F32) * flags[column, k, pairs + p]
            total = term if total is None else total + term
        return total.astype(BF16)

    def solved_ready(a):
        wait(solved.at[a, pl.ds(0, nx - 1)], xa_r.at[a])

    def spread_solved(a, b):
        p = pair_index(a, b)

        def go(k):
            peer = wrap(c + k, nc)
            pick_out[p, k - 1] = choose(peer, a, p)
            send(
                pick_out.at[p, k - 1], pick_in.at[p, k - 1], xb_s.at[p], xb_r.at[p], row, peer
            )

        each(nc, go)
        pick_own[p] = choose(c, a, p)

    def gather_solved(a, b):
        p = pair_index(a, b)
        wait(pick_in.at[p], xb_r.at[p])
        source = pick_own[p]
        for k in range(nc - 1):
            source = source + pick_in[p, k]
        wait(u_home.at[p, pl.ds(0, width - step)], ua_r.at[p])
        return product(source, u_home[p])

    idx = pair_index
    for p in order:
        lower_to_columns(p)
    flags_to_home()
    wait(rhs_home, rhs_r)
    solve_lower(0, rhs_home[0])
    lower_to_home(idx(1, 0))
    upper_over_x(idx(3, 2))
    lower_to_home(idx(2, 0))
    lower_to_home(idx(2, 1))
    contribute(1, 0)
    flags_ready()
    for b in range(3):
        lower_to_home(idx(3, b))
    spread_parts(1)
    contribute(2, 0)
    upper_over_x(idx(2, 1))
    upper_over_z(idx(3, 2))
    solve_lower(1, collect_parts(1))
    contribute(2, 1)
    upper_over_x(idx(3, 1))
    spread_parts(2)
    contribute(3, 0)
    contribute(3, 1)
    upper_to_all(idx(3, 2))
    upper_over_z(idx(2, 1))
    solve_lower(2, collect_parts(2))
    contribute(3, 2)
    upper_over_x(idx(1, 0))
    spread_parts(3)
    upper_over_z(idx(3, 1))
    upper_to_all(idx(2, 1))
    solve_lower(3, collect_parts(3))
    solve_upper(3, fwd[3])
    upper_over_x(idx(2, 0))
    upper_over_z(idx(1, 0))
    upper_to_all(idx(3, 1))
    solved_ready(3)
    spread_solved(3, 2)
    spread_solved(3, 1)
    spread_solved(3, 0)
    upper_over_x(idx(3, 0))
    total = gather_solved(3, 2)
    solve_upper(2, (fwd[2].astype(F32) - total).astype(BF16))
    upper_over_z(idx(2, 0))
    upper_to_all(idx(1, 0))
    solved_ready(2)
    spread_solved(2, 1)
    spread_solved(2, 0)
    total = gather_solved(3, 1)
    total = total + gather_solved(2, 1)
    solve_upper(1, (fwd[1].astype(F32) - total).astype(BF16))
    upper_over_z(idx(3, 0))
    upper_to_all(idx(2, 0))
    solved_ready(1)
    spread_solved(1, 0)
    upper_to_all(idx(3, 0))
    total = gather_solved(3, 0)
    total = total + gather_solved(2, 0)
    total = total + gather_solved(1, 0)
    solve_upper(0, (fwd[0].astype(F32) - total).astype(BF16))

    for p in range(pairs):
        wait(l_in.at[p], ly_s.at[p])
        wait(u_in.at[p], ux_s.at[p])
        wait(u_slice.at[p], uz_s.at[p])
        wait(u_slice.at[p], ua_s.at[p])
        wait(near.at[p, pl.ds(0, nx - 1)], na_s.at[p])
        wait(pick_in.at[p], xb_s.at[p])
    for l in range(lev - 1):
        wait(part_in.at[l], pb_s.at[l])
        wait(solved.at[l + 1, pl.ds(0, nx - 1)], xa_s.at[l + 1])
    wait(flag_x.at[pl.ds(0, nx - 1)], fx_s)
    wait(rhs_home.at[pl.ds(0, nx - 1)] if lev == nx else rhs.at[pl.ds(0, nx - 1)], rhs_s)

    @pl.when(diagonal)
    def _():
        for p in range(pairs):
            wait(l_home.at[p, pl.ds(0, width - step)], ld_s.at[p])
        wait(flag_all.at[pl.ds(0, nz - 1)], fd_s)

    @pl.when(jnp.logical_not(diagonal))
    def _():
        for p in range(pairs):
            wait(l_home.at[p], ld_s.at[p])
        wait(flag_all, fd_s)

    for l in range(lev):
        wait(out.at[l, pl.ds(0, nx - 1)], out_s.at[l])
        wait(out.at[l], out_r.at[l])


def per_device(
    right_sides, lower_blocks, lower_fill, upper_blocks, upper_fill, lower_inv, upper_inv
):
    lev, rows, nx, width = right_sides.shape
    nc = lax.axis_size("col")
    pairs = lev * (lev - 1) // 2
    step = width // nc
    wide = rows * nx
    by_target = jnp.transpose(right_sides, (2, 0, 1, 3))

    def vmem(shape, dtype=BF16):
        return pltpu.VMEM(shape, dtype)

    def dma(*shape):
        return pltpu.SemaphoreType.DMA(shape)

    square = (width, width)
    block = (wide, width)
    scratch = [
        vmem((pairs, nx) + square),
        vmem((pairs, nx) + square),
        vmem((lev,) + square),
        vmem((lev,) + square),
        vmem((pairs,) + square),
        vmem((pairs, nc - 1, step, width)),
        vmem((pairs, step, width)),
        vmem((pairs,) + square),
        vmem((pairs, nx - 1) + square),
        vmem((pairs,) + square),
        vmem((pairs, nc - 1, step, width)),
        vmem((pairs,) + square),
        vmem((lev,) + block),
        vmem((lev,) + block),
        vmem((nx, 8, 128), F32),
        vmem((nx, 8, 128), F32),
        vmem((8, 128), F32),
        vmem((nc, 8, 128), F32),
        pltpu.SMEM((nc, 8, 128), F32),
        vmem((pairs, nx) + block),
        vmem((lev - 1, nc - 1) + block),
        vmem((lev - 1, nc - 1) + block),
        vmem((lev, nx) + block),
        vmem((pairs, nc - 1) + block),
        vmem((pairs, nc - 1) + block),
        vmem((pairs,) + block),
        vmem((lev,) + block, F32),
        dma(2 * pairs),
        dma(2 * lev),
        pltpu.SemaphoreType.DMA,
    ]
    scratch += [pltpu.SemaphoreType.DMA] * 6
    scratch += [dma(pairs)] * 12
    scratch += [dma(lev - 1)] * 2
    scratch += [dma(lev)] * 2
    scratch += [dma(pairs)] * 2
    scratch += [dma(lev)] * 2
    anywhere = pl.BlockSpec(memory_space=pl.ANY)
    scalars = pl.BlockSpec(memory_space=pltpu.SMEM)
    result = pl.pallas_call(
        functools.partial(sweep_kernel, (lev, nx, nc, rows, width)),
        out_shape=jax.ShapeDtypeStruct((lev, nx, rows, width), F32),
        in_specs=[anywhere, anywhere, scalars, anywhere, scalars, anywhere, anywhere],
        out_specs=anywhere,
        scratch_shapes=scratch,
        compiler_params=pltpu.CompilerParams(
            collective_id=0, has_side_effects=True, vmem_limit_bytes=48 * 1024 * 1024
        ),
    )(by_target, lower_blocks, lower_fill, upper_blocks, upper_fill, lower_inv, upper_inv)
    return jnp.transpose(result, (0, 2, 1, 3))


def solution(mesh):
    placed = (
        P(None, "row", "col", None),
        P(None, "col", "row", None, None),
        P(None, "col", "row"),
        P(None, "col", "row", None, None),
        P(None, "col", "row"),
        P(None, "col", None, None),
        P(None, "col", None, None),
    )
    return jax.shard_map(
        per_device,
        mesh=mesh,
        in_specs=placed,
        out_specs=P(None, "row", "col", None),
        check_vma=False,
    )
```

```python
import functools

import jax
import jax.numpy as jnp
from jax import lax
from jax.experimental import pallas as pl
from jax.experimental.pallas import tpu as pltpu
from jax.sharding import PartitionSpec as P

MESH = pl.DeviceIdType.MESH
F32 = jnp.float32
BF16 = jnp.bfloat16
PARTS = 2


def pair_index(current, earlier):
    upper_level = max(current, earlier)
    lower_level = min(current, earlier)
    return upper_level * (upper_level - 1) // 2 + lower_level


def sweep_kernel(
    dims, rhs_raw, lower, lower_fill, upper, upper_fill, lower_inv, upper_inv, out,
    l_raw, u_raw, linv, uinv, l_loc, l_in, l_sum, l_home, u_in, u_sum, u_slice, u_home,
    rhs_home, fwd, flag_out, flag_x, flag_row, flag_all, flags,
    rhs_tile, rhs, raw_sem,
    near, part_out, part_in, solved, pick_out, pick_in, pick_own, answer,
    load_sem, inv_sem, flag_sem,
    rhs_s, rhs_r, fx_s, fx_r, fd_s, fd_r, ly_s, ly_r, ld_s, ld_r, ux_s, ux_r, uz_s, uz_r,
    ua_s, ua_r, na_s, na_r, pb_s, pb_r, xa_s, xa_r, xb_s, xb_r, out_s, out_r,
):
    lev, nx, nc, rows, width, parts = dims
    share = rows * nx // parts
    pairs = lev * (lev - 1) // 2
    nz = nc
    step = width // nc
    row = lax.axis_index("row")
    c = lax.axis_index("col")
    z = lax.div(row, nx)
    x = lax.rem(row, nx)
    diagonal = c == z

    def wrap(value, count):
        return lax.rem(value, count)

    def send(src, dst, ssem, rsem, to_row, to_col):
        pltpu.make_async_remote_copy(
            src_ref=src, dst_ref=dst, send_sem=ssem, recv_sem=rsem,
            device_id=(to_row, to_col), device_id_type=MESH,
        ).start()

    def wait(ref, sem):
        pltpu.make_async_copy(ref, ref, sem).wait()

    def x_peer(k):
        return z * nx + wrap(x + k, nx)

    def z_peer(k):
        return wrap(z + k, nz) * nx + x

    def each(count, body):
        def run(k, carry):
            body(k)
            return carry

        lax.fori_loop(1, count, run, 0)

    order = []
    for a in range(1, lev):
        for b in range(a):
            order.append(pair_index(a, b))
    back = []
    for b in range(lev - 2, -1, -1):
        for a in range(b + 1, lev):
            back.append(pair_index(a, b))

    def load_lower(p):
        return pltpu.make_async_copy(lower.at[p, :, 0], l_raw.at[p], load_sem.at[p])

    def load_upper(p):
        return pltpu.make_async_copy(upper.at[p, :, 0], u_raw.at[p], load_sem.at[pairs + p])

    def load_linv(l):
        return pltpu.make_async_copy(lower_inv.at[l, x], linv.at[l], inv_sem.at[l])

    def load_uinv(l):
        return pltpu.make_async_copy(upper_inv.at[l, x], uinv.at[l], inv_sem.at[lev + l])

    fetch = pltpu.make_async_copy(rhs_raw, rhs_tile, raw_sem)
    fetch.start()
    load_lower(order[0]).start()
    load_upper(back[0]).start()
    load_linv(0).start()
    load_upper(back[1]).start()
    for p in order[1:]:
        load_lower(p).start()
    for l in range(1, lev):
        load_linv(l).start()
    for p in back[2:]:
        load_upper(p).start()
    for l in range(lev - 1, -1, -1):
        load_uinv(l).start()

    barrier = pltpu.get_barrier_semaphore()

    def greet(to_row, to_col):
        pl.semaphore_signal(barrier, inc=1, device_id=(to_row, to_col), device_id_type=MESH)

    each(nx, lambda k: greet(x_peer(k), c))
    each(nc, lambda k: greet(row, wrap(c + k, nc)))
    each(nz, lambda k: greet(z_peer(k), c))

    def greet_diagonal(cc):
        @pl.when(jnp.logical_not(jnp.logical_and(diagonal, cc == c)))
        def _():
            greet(c * nx + x, cc)

    def greet_run(k, carry):
        greet_diagonal(k)
        return carry

    lax.fori_loop(0, nc, greet_run, 0)

    fetch.wait()
    for l in range(lev):
        for t in range(nx):
            rhs[t, l] = rhs_tile[l, :, t, :]

    lane = lax.broadcasted_iota(jnp.int32, (8, 128), 1)
    for t in range(nx):
        tile = jnp.zeros((8, 128), F32)
        for p in range(pairs):
            tile = jnp.where(lane == p, lower_fill[t, 0, p].astype(F32), tile)
            tile = jnp.where(lane == pairs + p, upper_fill[t, 0, p].astype(F32), tile)
        flag_out[t] = tile
    flag_x[x] = flag_out[x]

    pl.semaphore_wait(barrier, (nx - 1) + (nc - 1) + (nz - 1) + nc - diagonal.astype(jnp.int32))

    own_rows = pl.ds(pl.multiple_of(x * rows, rows), rows)

    def start_x(k):
        target = wrap(x + k, nx)
        send(flag_out.at[target], flag_x.at[x], fx_s, fx_r, x_peer(k), c)
        send(rhs.at[target], rhs_home.at[:, own_rows, :], rhs_s, rhs_r, x_peer(k), c)

    each(nx, start_x)
    pltpu.make_async_copy(rhs.at[x], rhs_home.at[:, own_rows, :], rhs_r).start()

    def chunk(index):
        return pl.ds(pl.multiple_of(index * step, step), step)

    def lower_to_columns(p):
        load_lower(p).wait()
        found = jnp.zeros((width, width), BF16)
        for t in range(nx):
            found = lax.select(lower_fill[t, 0, p] != 0, l_raw[p, t], found)
        l_loc[p] = found

        def go(k):
            peer = wrap(c + k, nc)
            send(l_loc.at[p, chunk(peer)], l_in.at[p, k - 1], ly_s.at[p], ly_r.at[p], row, peer)

        each(nc, go)

    def over_z(body):
        def run(zz, carry):
            same = jnp.logical_and(zz == z, diagonal)

            @pl.when(same)
            def _():
                body(zz, True)

            @pl.when(jnp.logical_not(same))
            def _():
                body(zz, False)

            return carry

        lax.fori_loop(0, nz, run, 0)

    def lower_to_home(p):
        wait(l_in.at[p], ly_r.at[p])
        total = l_loc[p, chunk(c), :]
        for k in range(nc - 1):
            total = total + l_in[p, k]
        l_sum[p] = total

        def go(zz, same):
            if same:
                pltpu.make_async_copy(l_sum.at[p], l_home.at[p, chunk(c)], ld_r.at[p]).start()
            else:
                send(
                    l_sum.at[p], l_home.at[p, chunk(c)], ld_s.at[p], ld_r.at[p],
                    zz * nx + x, z,
                )

        over_z(go)

    def flags_to_home():
        wait(flag_x.at[pl.ds(0, nx - 1)], fx_r)
        sub = lax.broadcasted_iota(jnp.int32, (8, 128), 0)
        tile = jnp.zeros((8, 128), F32)
        for k in range(nx):
            tile = jnp.where(sub == k, flag_x[k], tile)
        flag_row[...] = tile

        def go(zz, same):
            if same:
                pltpu.make_async_copy(flag_row, flag_all.at[c], fd_r).start()
            else:
                send(flag_row, flag_all.at[c], fd_s, fd_r, zz * nx + x, z)

        over_z(go)

    def flags_ready():
        wait(flag_all, fd_r)
        copy = pltpu.make_async_copy(flag_all, flags, flag_sem)
        copy.start()
        copy.wait()

    def upper_over_x(p):
        load_upper(p).wait()
        for t in range(nx):
            u_raw[p, t] = lax.select(
                upper_fill[t, 0, p] != 0, u_raw[p, t], jnp.zeros((width, width), BF16)
            )

        def go(k):
            send(u_raw.at[p, wrap(x + k, nx)], u_in.at[p, k - 1], ux_s.at[p], ux_r.at[p], x_peer(k), c)

        each(nx, go)

    def upper_over_z(p):
        wait(u_in.at[p], ux_r.at[p])
        total = u_raw[p, x]
        for k in range(nx - 1):
            total = total + u_in[p, k]
        u_sum[p] = total

        def go(k):
            send(
                u_sum.at[p, chunk(wrap(z + k, nz))], u_slice.at[p, k - 1], uz_s.at[p], uz_r.at[p],
                z_peer(k), c,
            )

        each(nz, go)

    def upper_to_all(p):
        wait(u_slice.at[p], uz_r.at[p])
        total = u_sum[p, chunk(z), :]
        for k in range(nz - 1):
            total = total + u_slice[p, k]
        u_home[p, chunk(z), :] = total

        def go(k):
            send(u_home.at[p, chunk(z)], u_home.at[p, chunk(z)], ua_s.at[p], ua_r.at[p], z_peer(k), c)

        each(nz, go)

    def product(left, right):
        return jnp.dot(left, right, preferred_element_type=F32)

    def over_parts(body):
        def run(h, carry):
            body(h)
            return carry

        lax.fori_loop(0, parts, run, 0)

    def part_rows(h):
        return pl.ds(pl.multiple_of(h * share, share), share)

    def lower_ready(p):
        wait(l_home.at[p], ld_r.at[p])

    def contribute(h, a, b):
        p = pair_index(a, b)
        near[h, p, x] = product(fwd[b, part_rows(h), :], l_home[p]).astype(BF16)

        def go(k):
            send(
                near.at[h, p, x], near.at[h, p, x], na_s.at[h, p], na_r.at[h, p], x_peer(k), c
            )

        each(nx, go)

    def mix(h, column, level):
        total = None
        for m in range(level):
            p = pair_index(level, m)
            for k in range(nx):
                term = near[h, p, k].astype(F32) * flags[column, k, p]
                total = term if total is None else total + term
        return total

    def spread_parts(h, level):
        for m in range(level):
            p = pair_index(level, m)
            wait(near.at[h, p, pl.ds(0, nx - 1)], na_r.at[h, p])

        def go(k):
            peer = wrap(c + k, nc)
            part_out[h, level - 1, k - 1] = mix(h, peer, level).astype(BF16)
            send(
                part_out.at[h, level - 1, k - 1], part_in.at[h, level - 1, k - 1],
                pb_s.at[h, level - 1], pb_r.at[h, level - 1], row, peer,
            )

        each(nc, go)

    def collect_parts(h, level):
        total = mix(h, c, level)
        wait(part_in.at[h, level - 1], pb_r.at[h, level - 1])
        for k in range(nc - 1):
            total = total + part_in[h, level - 1, k].astype(F32)
        return (rhs_home[level, part_rows(h), :].astype(F32) - total).astype(BF16)

    def solve_lower(h, level, residual):
        fwd[level, part_rows(h), :] = product(residual, linv[level]).astype(BF16)

    def solve_upper(h, level, residual):
        result = product(residual, uinv[level])
        if level:
            solved[h, level, x] = result.astype(BF16)

            def go(k):
                send(
                    solved.at[h, level, x], solved.at[h, level, x],
                    xa_s.at[h, level], xa_r.at[h, level], x_peer(k), c,
                )

            each(nx, go)
        answer[level, part_rows(h), :] = result

    def give_answer(level):
        def go(k):
            target = wrap(x + k, nx)
            there = pl.ds(pl.multiple_of(target * rows, rows), rows)
            send(
                answer.at[level, there], out.at[level, x], out_s.at[level], out_r.at[level],
                x_peer(k), c,
            )

        each(nx, go)
        pltpu.make_async_copy(answer.at[level, own_rows], out.at[level, x], out_r.at[level]).start()

    def choose(h, column, a, p):
        total = None
        for k in range(nx):
            term = solved[h, a, k].astype(F32) * flags[column, k, pairs + p]
            total = term if total is None else total + term
        return total.astype(BF16)

    def solved_ready(h, a):
        wait(solved.at[h, a, pl.ds(0, nx - 1)], xa_r.at[h, a])

    def spread_solved(h, a, b):
        p = pair_index(a, b)

        def go(k):
            peer = wrap(c + k, nc)
            pick_out[h, p, k - 1] = choose(h, peer, a, p)
            send(
                pick_out.at[h, p, k - 1], pick_in.at[h, p, k - 1],
                xb_s.at[h, p], xb_r.at[h, p], row, peer,
            )

        each(nc, go)
        pick_own[h, p] = choose(h, c, a, p)

    def upper_ready(p):
        wait(u_home.at[p, pl.ds(0, width - step)], ua_r.at[p])

    def gather_solved(h, a, b):
        p = pair_index(a, b)
        wait(pick_in.at[h, p], xb_r.at[h, p])
        source = pick_own[h, p]
        for k in range(nc - 1):
            source = source + pick_in[h, p, k]
        return product(source, u_home[p])

    def first_level(h):
        solve_lower(h, 0, rhs_home[0, part_rows(h), :])

    def next_level(level):
        load_linv(level).wait()
        lower_ready(pair_index(level + 1, level))

        def body(h):
            solve_lower(h, level, collect_parts(h, level))
            contribute(h, level + 1, level)

        over_parts(body)

    def back_level(level):
        load_uinv(level).wait()
        for a in range(level + 1, lev):
            upper_ready(pair_index(a, level))

        def body(h):
            total = None
            for a in range(lev - 1, level, -1):
                term = gather_solved(h, a, level)
                total = term if total is None else total + term
            residual = (fwd[level, part_rows(h), :].astype(F32) - total).astype(BF16)
            solve_upper(h, level, residual)

        over_parts(body)
        give_answer(level)

    def turn(h):
        solve_lower(h, 3, collect_parts(h, 3))
        solve_upper(h, 3, fwd[3, part_rows(h), :])

    def pass_up(a, b):
        lower_ready(pair_index(a, b))
        over_parts(lambda h: contribute(h, a, b))

    def pass_down(a, b, arrived=False):
        def body(h):
            if arrived:
                solved_ready(h, a)
            spread_solved(h, a, b)

        over_parts(body)

    idx = pair_index
    lower_to_columns(idx(1, 0))
    upper_over_x(idx(3, 2))
    flags_to_home()
    wait(rhs_home, rhs_r)
    load_linv(0).wait()
    over_parts(first_level)
    lower_to_home(idx(1, 0))
    lower_to_columns(idx(2, 0))
    lower_to_columns(idx(2, 1))
    upper_over_x(idx(2, 1))
    lower_to_home(idx(2, 0))
    lower_to_home(idx(2, 1))
    pass_up(1, 0)
    flags_ready()
    for b in range(3):
        lower_to_columns(idx(3, b))
    upper_over_z(idx(3, 2))
    over_parts(lambda h: spread_parts(h, 1))
    upper_over_x(idx(3, 1))
    next_level(1)
    for b in range(3):
        lower_to_home(idx(3, b))
    pass_up(2, 0)
    upper_over_z(idx(2, 1))
    over_parts(lambda h: spread_parts(h, 2))
    upper_over_x(idx(1, 0))
    upper_to_all(idx(3, 2))
    next_level(2)
    pass_up(3, 0)
    pass_up(3, 1)
    upper_over_z(idx(3, 1))
    upper_to_all(idx(2, 1))
    over_parts(lambda h: spread_parts(h, 3))
    upper_over_x(idx(2, 0))
    load_linv(3).wait()
    load_uinv(3).wait()
    over_parts(turn)
    give_answer(3)
    upper_over_z(idx(1, 0))
    upper_to_all(idx(3, 1))
    pass_down(3, 2, True)
    upper_over_x(idx(3, 0))
    pass_down(3, 1)
    upper_over_z(idx(2, 0))
    back_level(2)
    upper_to_all(idx(1, 0))
    pass_down(2, 1, True)
    pass_down(3, 0)
    upper_over_z(idx(3, 0))
    upper_to_all(idx(2, 0))
    back_level(1)
    pass_down(2, 0)
    upper_to_all(idx(3, 0))
    pass_down(1, 0, True)
    back_level(0)

    for p in range(pairs):
        wait(l_in.at[p], ly_s.at[p])
        wait(u_in.at[p], ux_s.at[p])
        wait(u_slice.at[p], uz_s.at[p])
        wait(u_slice.at[p], ua_s.at[p])
        for h in range(parts):
            wait(near.at[h, p, pl.ds(0, nx - 1)], na_s.at[h, p])
            wait(pick_in.at[h, p], xb_s.at[h, p])
    for l in range(lev - 1):
        for h in range(parts):
            wait(part_in.at[h, l], pb_s.at[h, l])
            wait(solved.at[h, l + 1, pl.ds(0, nx - 1)], xa_s.at[h, l + 1])
    wait(flag_x.at[pl.ds(0, nx - 1)], fx_s)
    wait(rhs_home.at[pl.ds(0, nx - 1)] if lev == nx else rhs.at[pl.ds(0, nx - 1)], rhs_s)

    @pl.when(diagonal)
    def _():
        for p in range(pairs):
            wait(l_home.at[p, pl.ds(0, width - step)], ld_s.at[p])
        wait(flag_all.at[pl.ds(0, nz - 1)], fd_s)

    @pl.when(jnp.logical_not(diagonal))
    def _():
        for p in range(pairs):
            wait(l_home.at[p], ld_s.at[p])
        wait(flag_all, fd_s)

    for l in range(lev):
        wait(out.at[l, pl.ds(0, nx - 1)], out_s.at[l])
        wait(out.at[l], out_r.at[l])


def per_device(
    right_sides, lower_blocks, lower_fill, upper_blocks, upper_fill, lower_inv, upper_inv
):
    lev, rows, nx, width = right_sides.shape
    nc = lax.axis_size("col")
    pairs = lev * (lev - 1) // 2
    step = width // nc
    wide = rows * nx

    def vmem(shape, dtype=BF16):
        return pltpu.VMEM(shape, dtype)

    def dma(*shape):
        return pltpu.SemaphoreType.DMA(shape)

    square = (width, width)
    block = (wide, width)
    part = (wide // PARTS, width)
    scratch = [
        vmem((pairs, nx) + square),
        vmem((pairs, nx) + square),
        vmem((lev,) + square),
        vmem((lev,) + square),
        vmem((pairs,) + square),
        vmem((pairs, nc - 1, step, width)),
        vmem((pairs, step, width)),
        vmem((pairs,) + square),
        vmem((pairs, nx - 1) + square),
        vmem((pairs,) + square),
        vmem((pairs, nc - 1, step, width)),
        vmem((pairs,) + square),
        vmem((lev,) + block),
        vmem((lev,) + block),
        vmem((nx, 8, 128), F32),
        vmem((nx, 8, 128), F32),
        vmem((8, 128), F32),
        vmem((nc, 8, 128), F32),
        pltpu.SMEM((nc, 8, 128), F32),
        vmem((lev, rows, nx, width)),
        vmem((nx, lev, rows, width)),
        pltpu.SemaphoreType.DMA,
        vmem((PARTS, pairs, nx) + part),
        vmem((PARTS, lev - 1, nc - 1) + part),
        vmem((PARTS, lev - 1, nc - 1) + part),
        vmem((PARTS, lev, nx) + part),
        vmem((PARTS, pairs, nc - 1) + part),
        vmem((PARTS, pairs, nc - 1) + part),
        vmem((PARTS, pairs) + part),
        vmem((lev,) + block, F32),
        dma(2 * pairs),
        dma(2 * lev),
        pltpu.SemaphoreType.DMA,
    ]
    scratch += [pltpu.SemaphoreType.DMA] * 6
    scratch += [dma(pairs)] * 10
    scratch += [dma(PARTS, pairs)] * 2
    scratch += [dma(PARTS, lev - 1)] * 2
    scratch += [dma(PARTS, lev)] * 2
    scratch += [dma(PARTS, pairs)] * 2
    scratch += [dma(lev)] * 2
    anywhere = pl.BlockSpec(memory_space=pl.ANY)
    scalars = pl.BlockSpec(memory_space=pltpu.SMEM)
    result = pl.pallas_call(
        functools.partial(sweep_kernel, (lev, nx, nc, rows, width, PARTS)),
        out_shape=jax.ShapeDtypeStruct((lev, nx, rows, width), F32),
        in_specs=[anywhere, anywhere, scalars, anywhere, scalars, anywhere, anywhere],
        out_specs=anywhere,
        scratch_shapes=scratch,
        compiler_params=pltpu.CompilerParams(
            collective_id=0, has_side_effects=True, vmem_limit_bytes=60 * 1024 * 1024
        ),
    )(
        right_sides, lower_blocks, jnp.transpose(lower_fill, (1, 2, 0)),
        upper_blocks, jnp.transpose(upper_fill, (1, 2, 0)), lower_inv, upper_inv,
    )
    return jnp.transpose(result, (0, 2, 1, 3))


def solution(mesh):
    placed = (
        P(None, "row", "col", None),
        P(None, "col", "row", None, None),
        P(None, "col", "row"),
        P(None, "col", "row", None, None),
        P(None, "col", "row"),
        P(None, "col", None, None),
        P(None, "col", None, None),
    )
    return jax.shard_map(
        per_device,
        mesh=mesh,
        in_specs=placed,
        out_specs=P(None, "row", "col", None),
        check_vma=False,
    )
```

```python
import functools

import jax
import jax.numpy as jnp
from jax import lax
from jax.experimental import pallas as pl
from jax.experimental.pallas import tpu as pltpu
from jax.sharding import PartitionSpec as P

MESH = pl.DeviceIdType.MESH
F32 = jnp.float32
BF16 = jnp.bfloat16
PARTS = 2


def pair_index(current, earlier):
    upper_level = max(current, earlier)
    lower_level = min(current, earlier)
    return upper_level * (upper_level - 1) // 2 + lower_level


def sweep_kernel(
    dims, rhs_raw, lower, lower_fill, upper, upper_fill, lower_inv, upper_inv, out,
    l_raw, u_raw, linv, uinv, l_loc, l_in, l_sum, l_home, u_in, u_sum, u_slice, u_home,
    rhs_home, fwd, flag_out, flag_x, flag_row, flag_all, flags,
    rhs_tile, rhs, raw_sem,
    near, part_out, part_in, solved, pick_out, pick_in, pick_own, answer,
    load_sem, inv_sem, flag_sem,
    rhs_s, rhs_r, fx_s, fx_r, fd_s, fd_r, ly_s, ly_r, ld_s, ld_r, ux_s, ux_r, uz_s, uz_r,
    ua_s, ua_r, na_s, na_r, pb_s, pb_r, xa_s, xa_r, xb_s, xb_r, out_s, out_r,
):
    lev, nx, nc, rows, width, parts = dims
    share = rows * nx // parts
    pairs = lev * (lev - 1) // 2
    nz = nc
    step = width // nc
    row = lax.axis_index("row")
    c = lax.axis_index("col")
    z = lax.div(row, nx)
    x = lax.rem(row, nx)
    diagonal = c == z

    def wrap(value, count):
        return lax.rem(value, count)

    def send(src, dst, ssem, rsem, to_row, to_col):
        pltpu.make_async_remote_copy(
            src_ref=src, dst_ref=dst, send_sem=ssem, recv_sem=rsem,
            device_id=(to_row, to_col), device_id_type=MESH,
        ).start()

    def wait(ref, sem):
        pltpu.make_async_copy(ref, ref, sem).wait()

    def x_peer(k):
        return z * nx + wrap(x + k, nx)

    def z_peer(k):
        return wrap(z + k, nz) * nx + x

    def each(count, body):
        def run(k, carry):
            body(k)
            return carry

        lax.fori_loop(1, count, run, 0)

    order = []
    for a in range(1, lev):
        for b in range(a):
            order.append(pair_index(a, b))
    back = []
    for b in range(lev - 2, -1, -1):
        for a in range(b + 1, lev):
            back.append(pair_index(a, b))

    def load_lower(p):
        return pltpu.make_async_copy(lower.at[p, :, 0], l_raw.at[p], load_sem.at[p])

    def load_upper(p):
        return pltpu.make_async_copy(upper.at[p, :, 0], u_raw.at[p], load_sem.at[pairs + p])

    def load_linv(l):
        return pltpu.make_async_copy(lower_inv.at[l, x], linv.at[l], inv_sem.at[l])

    def load_uinv(l):
        return pltpu.make_async_copy(upper_inv.at[l, x], uinv.at[l], inv_sem.at[lev + l])

    fetch = pltpu.make_async_copy(rhs_raw, rhs_tile, raw_sem)
    fetch.start()
    load_lower(order[0]).start()
    load_upper(back[0]).start()
    load_linv(0).start()
    load_upper(back[1]).start()
    for p in order[1:]:
        load_lower(p).start()
    for l in range(1, lev):
        load_linv(l).start()
    for p in back[2:]:
        load_upper(p).start()
    for l in range(lev - 1, -1, -1):
        load_uinv(l).start()

    barrier = pltpu.get_barrier_semaphore()

    def greet(to_row, to_col):
        pl.semaphore_signal(barrier, inc=1, device_id=(to_row, to_col), device_id_type=MESH)

    each(nx, lambda k: greet(x_peer(k), c))
    each(nc, lambda k: greet(row, wrap(c + k, nc)))
    each(nz, lambda k: greet(z_peer(k), c))

    def greet_diagonal(cc):
        @pl.when(jnp.logical_not(jnp.logical_and(diagonal, cc == c)))
        def _():
            greet(c * nx + x, cc)

    def greet_run(k, carry):
        greet_diagonal(k)
        return carry

    lax.fori_loop(0, nc, greet_run, 0)

    fetch.wait()
    for l in range(lev):
        for t in range(nx):
            rhs[t, l] = rhs_tile[l, :, t, :]

    lane = lax.broadcasted_iota(jnp.int32, (8, 128), 1)
    for t in range(nx):
        tile = jnp.zeros((8, 128), F32)
        for p in range(pairs):
            tile = jnp.where(lane == p, lower_fill[t, 0, p].astype(F32), tile)
            tile = jnp.where(lane == pairs + p, upper_fill[t, 0, p].astype(F32), tile)
        flag_out[t] = tile
    flag_x[x] = flag_out[x]

    pl.semaphore_wait(barrier, (nx - 1) + (nc - 1) + (nz - 1) + nc - diagonal.astype(jnp.int32))

    own_rows = pl.ds(pl.multiple_of(x * rows, rows), rows)

    def start_x(k):
        target = wrap(x + k, nx)
        send(flag_out.at[target], flag_x.at[x], fx_s, fx_r, x_peer(k), c)
        send(rhs.at[target], rhs_home.at[:, own_rows, :], rhs_s, rhs_r, x_peer(k), c)

    each(nx, start_x)
    pltpu.make_async_copy(rhs.at[x], rhs_home.at[:, own_rows, :], rhs_r).start()

    def chunk(index):
        return pl.ds(pl.multiple_of(index * step, step), step)

    def lower_to_columns(p):
        load_lower(p).wait()
        found = jnp.zeros((width, width), BF16)
        for t in range(nx):
            found = lax.select(lower_fill[t, 0, p] != 0, l_raw[p, t], found)
        l_loc[p] = found

        def go(k):
            peer = wrap(c + k, nc)
            send(l_loc.at[p, chunk(peer)], l_in.at[p, k - 1], ly_s.at[p], ly_r.at[p], row, peer)

        each(nc, go)

    def over_z(body):
        def run(zz, carry):
            same = jnp.logical_and(zz == z, diagonal)

            @pl.when(same)
            def _():
                body(zz, True)

            @pl.when(jnp.logical_not(same))
            def _():
                body(zz, False)

            return carry

        lax.fori_loop(0, nz, run, 0)

    def lower_to_home(p):
        wait(l_in.at[p], ly_r.at[p])
        total = l_loc[p, chunk(c), :]
        for k in range(nc - 1):
            total = total + l_in[p, k]
        l_sum[p] = total

        def go(zz, same):
            if same:
                pltpu.make_async_copy(l_sum.at[p], l_home.at[p, chunk(c)], ld_r.at[p]).start()
            else:
                send(
                    l_sum.at[p], l_home.at[p, chunk(c)], ld_s.at[p], ld_r.at[p],
                    zz * nx + x, z,
                )

        over_z(go)

    def flags_to_home():
        wait(flag_x.at[pl.ds(0, nx - 1)], fx_r)
        sub = lax.broadcasted_iota(jnp.int32, (8, 128), 0)
        tile = jnp.zeros((8, 128), F32)
        for k in range(nx):
            tile = jnp.where(sub == k, flag_x[k], tile)
        flag_row[...] = tile

        def go(zz, same):
            if same:
                pltpu.make_async_copy(flag_row, flag_all.at[c], fd_r).start()
            else:
                send(flag_row, flag_all.at[c], fd_s, fd_r, zz * nx + x, z)

        over_z(go)

    def flags_ready():
        wait(flag_all, fd_r)
        copy = pltpu.make_async_copy(flag_all, flags, flag_sem)
        copy.start()
        copy.wait()

    def upper_over_x(p):
        load_upper(p).wait()
        for t in range(nx):
            u_raw[p, t] = lax.select(
                upper_fill[t, 0, p] != 0, u_raw[p, t], jnp.zeros((width, width), BF16)
            )

        def go(k):
            send(u_raw.at[p, wrap(x + k, nx)], u_in.at[p, k - 1], ux_s.at[p], ux_r.at[p], x_peer(k), c)

        each(nx, go)

    def upper_over_z(p):
        wait(u_in.at[p], ux_r.at[p])
        total = u_raw[p, x]
        for k in range(nx - 1):
            total = total + u_in[p, k]
        u_sum[p] = total

        def go(k):
            send(
                u_sum.at[p, chunk(wrap(z + k, nz))], u_slice.at[p, k - 1], uz_s.at[p], uz_r.at[p],
                z_peer(k), c,
            )

        each(nz, go)

    def upper_to_all(p):
        wait(u_slice.at[p], uz_r.at[p])
        total = u_sum[p, chunk(z), :]
        for k in range(nz - 1):
            total = total + u_slice[p, k]
        u_home[p, chunk(z), :] = total

        def go(k):
            send(u_home.at[p, chunk(z)], u_home.at[p, chunk(z)], ua_s.at[p], ua_r.at[p], z_peer(k), c)

        each(nz, go)

    def product(left, right):
        return jnp.dot(left, right, preferred_element_type=F32)

    def over_parts(body):
        def run(h, carry):
            body(h)
            return carry

        lax.fori_loop(0, parts, run, 0)

    def part_rows(h):
        return pl.ds(pl.multiple_of(h * share, share), share)

    def lower_ready(p):
        wait(l_home.at[p], ld_r.at[p])

    def contribute(h, a, b):
        p = pair_index(a, b)
        near[h, p, x] = product(fwd[b, part_rows(h), :], l_home[p]).astype(BF16)

        def go(k):
            send(
                near.at[h, p, x], near.at[h, p, x], na_s.at[h, p], na_r.at[h, p], x_peer(k), c
            )

        each(nx, go)

    def mix(h, column, level):
        total = None
        for m in range(level):
            p = pair_index(level, m)
            for k in range(nx):
                term = near[h, p, k].astype(F32) * flags[column, k, p]
                total = term if total is None else total + term
        return total

    def spread_parts(h, level):
        for m in range(level):
            p = pair_index(level, m)
            wait(near.at[h, p, pl.ds(0, nx - 1)], na_r.at[h, p])

        def go(k):
            peer = wrap(c + k, nc)
            part_out[h, level - 1, k - 1] = mix(h, peer, level).astype(BF16)
            send(
                part_out.at[h, level - 1, k - 1], part_in.at[h, level - 1, k - 1],
                pb_s.at[h, level - 1], pb_r.at[h, level - 1], row, peer,
            )

        each(nc, go)

    def collect_parts(h, level):
        total = mix(h, c, level)
        wait(part_in.at[h, level - 1], pb_r.at[h, level - 1])
        for k in range(nc - 1):
            total = total + part_in[h, level - 1, k].astype(F32)
        return (rhs_home[level, part_rows(h), :].astype(F32) - total).astype(BF16)

    def solve_lower(h, level, residual):
        fwd[level, part_rows(h), :] = product(residual, linv[level]).astype(BF16)

    def solve_upper(h, level, residual):
        result = product(residual, uinv[level])
        if level:
            solved[h, level, x] = result.astype(BF16)

            def go(k):
                send(
                    solved.at[h, level, x], solved.at[h, level, x],
                    xa_s.at[h, level], xa_r.at[h, level], x_peer(k), c,
                )

            each(nx, go)
        answer[level, part_rows(h), :] = result

    def give_answer(level):
        def go(k):
            target = wrap(x + k, nx)
            there = pl.ds(pl.multiple_of(target * rows, rows), rows)
            send(
                answer.at[level, there], out.at[level, x], out_s.at[level], out_r.at[level],
                x_peer(k), c,
            )

        each(nx, go)
        pltpu.make_async_copy(answer.at[level, own_rows], out.at[level, x], out_r.at[level]).start()

    def give_part(h):
        for u in range(nx // parts):
            target = h * (nx // parts) + u
            there = pl.ds(pl.multiple_of(target * rows, rows), rows)

            @pl.when(target == x)
            def _():
                pltpu.make_async_copy(answer.at[0, there], out.at[0, x], out_r.at[0]).start()

            @pl.when(target != x)
            def _():
                send(
                    answer.at[0, there], out.at[0, x], out_s.at[0], out_r.at[0],
                    z * nx + target, c,
                )

    def choose(h, column, a, p):
        total = None
        for k in range(nx):
            term = solved[h, a, k].astype(F32) * flags[column, k, pairs + p]
            total = term if total is None else total + term
        return total.astype(BF16)

    def solved_ready(h, a):
        wait(solved.at[h, a, pl.ds(0, nx - 1)], xa_r.at[h, a])

    def spread_solved(h, a, b):
        p = pair_index(a, b)

        def go(k):
            peer = wrap(c + k, nc)
            pick_out[h, p, k - 1] = choose(h, peer, a, p)
            send(
                pick_out.at[h, p, k - 1], pick_in.at[h, p, k - 1],
                xb_s.at[h, p], xb_r.at[h, p], row, peer,
            )

        each(nc, go)
        pick_own[h, p] = choose(h, c, a, p)

    def upper_ready(p):
        wait(u_home.at[p, pl.ds(0, width - step)], ua_r.at[p])

    def gather_solved(h, a, b):
        p = pair_index(a, b)
        wait(pick_in.at[h, p], xb_r.at[h, p])
        source = pick_own[h, p]
        for k in range(nc - 1):
            source = source + pick_in[h, p, k]
        return product(source, u_home[p])

    def first_level(h):
        solve_lower(h, 0, rhs_home[0, part_rows(h), :])

    def next_level(level):
        load_linv(level).wait()
        lower_ready(pair_index(level + 1, level))

        def body(h):
            solve_lower(h, level, collect_parts(h, level))
            contribute(h, level + 1, level)

        over_parts(body)

    def back_level(level):
        load_uinv(level).wait()
        for a in range(level + 1, lev):
            upper_ready(pair_index(a, level))

        def body(h):
            total = None
            for a in range(lev - 1, level, -1):
                term = gather_solved(h, a, level)
                total = term if total is None else total + term
            residual = (fwd[level, part_rows(h), :].astype(F32) - total).astype(BF16)
            solve_upper(h, level, residual)
            if not level:
                give_part(h)

        over_parts(body)
        if level:
            give_answer(level)

    def turn(h):
        solve_lower(h, 3, collect_parts(h, 3))
        solve_upper(h, 3, fwd[3, part_rows(h), :])

    def pass_up(a, b):
        lower_ready(pair_index(a, b))
        over_parts(lambda h: contribute(h, a, b))

    def pass_down(a, b, arrived=False):
        def body(h):
            if arrived:
                solved_ready(h, a)
            spread_solved(h, a, b)

        over_parts(body)

    idx = pair_index
    lower_to_columns(idx(1, 0))
    upper_over_x(idx(3, 2))
    flags_to_home()
    wait(rhs_home, rhs_r)
    load_linv(0).wait()
    over_parts(first_level)
    lower_to_home(idx(1, 0))
    lower_to_columns(idx(2, 0))
    lower_to_columns(idx(2, 1))
    for b in range(3):
        lower_to_columns(idx(3, b))
    upper_over_x(idx(2, 1))
    lower_to_home(idx(2, 0))
    lower_to_home(idx(2, 1))
    pass_up(1, 0)
    lower_to_home(idx(3, 0))
    flags_ready()
    upper_over_z(idx(3, 2))
    over_parts(lambda h: spread_parts(h, 1))
    upper_over_x(idx(3, 1))
    next_level(1)
    lower_to_home(idx(3, 1))
    lower_to_home(idx(3, 2))
    pass_up(2, 0)
    upper_over_z(idx(2, 1))
    over_parts(lambda h: spread_parts(h, 2))
    upper_over_x(idx(1, 0))
    upper_to_all(idx(3, 2))
    next_level(2)
    pass_up(3, 0)
    pass_up(3, 1)
    upper_over_z(idx(3, 1))
    upper_to_all(idx(2, 1))
    over_parts(lambda h: spread_parts(h, 3))
    upper_over_x(idx(2, 0))
    load_linv(3).wait()
    load_uinv(3).wait()
    over_parts(turn)
    give_answer(3)
    upper_over_z(idx(1, 0))
    upper_to_all(idx(3, 1))
    pass_down(3, 2, True)
    upper_over_x(idx(3, 0))
    pass_down(3, 1)
    upper_over_z(idx(2, 0))
    back_level(2)
    upper_to_all(idx(1, 0))
    pass_down(2, 1, True)
    pass_down(3, 0)
    upper_over_z(idx(3, 0))
    upper_to_all(idx(2, 0))
    back_level(1)
    pass_down(2, 0)
    upper_to_all(idx(3, 0))
    pass_down(1, 0, True)
    back_level(0)

    for p in range(pairs):
        wait(l_in.at[p], ly_s.at[p])
        wait(u_in.at[p], ux_s.at[p])
        wait(u_slice.at[p], uz_s.at[p])
        wait(u_slice.at[p], ua_s.at[p])
        for h in range(parts):
            wait(near.at[h, p, pl.ds(0, nx - 1)], na_s.at[h, p])
            wait(pick_in.at[h, p], xb_s.at[h, p])
    for l in range(lev - 1):
        for h in range(parts):
            wait(part_in.at[h, l], pb_s.at[h, l])
            wait(solved.at[h, l + 1, pl.ds(0, nx - 1)], xa_s.at[h, l + 1])
    wait(flag_x.at[pl.ds(0, nx - 1)], fx_s)
    wait(rhs_home.at[pl.ds(0, nx - 1)] if lev == nx else rhs.at[pl.ds(0, nx - 1)], rhs_s)

    @pl.when(diagonal)
    def _():
        for p in range(pairs):
            wait(l_home.at[p, pl.ds(0, width - step)], ld_s.at[p])
        wait(flag_all.at[pl.ds(0, nz - 1)], fd_s)

    @pl.when(jnp.logical_not(diagonal))
    def _():
        for p in range(pairs):
            wait(l_home.at[p], ld_s.at[p])
        wait(flag_all, fd_s)

    for l in range(lev):
        wait(out.at[l, pl.ds(0, nx - 1)], out_s.at[l])
        wait(out.at[l], out_r.at[l])


def per_device(
    right_sides, lower_blocks, lower_fill, upper_blocks, upper_fill, lower_inv, upper_inv
):
    lev, rows, nx, width = right_sides.shape
    nc = lax.axis_size("col")
    pairs = lev * (lev - 1) // 2
    step = width // nc
    wide = rows * nx

    def vmem(shape, dtype=BF16):
        return pltpu.VMEM(shape, dtype)

    def dma(*shape):
        return pltpu.SemaphoreType.DMA(shape)

    square = (width, width)
    block = (wide, width)
    part = (wide // PARTS, width)
    scratch = [
        vmem((pairs, nx) + square),
        vmem((pairs, nx) + square),
        vmem((lev,) + square),
        vmem((lev,) + square),
        vmem((pairs,) + square),
        vmem((pairs, nc - 1, step, width)),
        vmem((pairs, step, width)),
        vmem((pairs,) + square),
        vmem((pairs, nx - 1) + square),
        vmem((pairs,) + square),
        vmem((pairs, nc - 1, step, width)),
        vmem((pairs,) + square),
        vmem((lev,) + block),
        vmem((lev,) + block),
        vmem((nx, 8, 128), F32),
        vmem((nx, 8, 128), F32),
        vmem((8, 128), F32),
        vmem((nc, 8, 128), F32),
        pltpu.SMEM((nc, 8, 128), F32),
        vmem((lev, rows, nx, width)),
        vmem((nx, lev, rows, width)),
        pltpu.SemaphoreType.DMA,
        vmem((PARTS, pairs, nx) + part),
        vmem((PARTS, lev - 1, nc - 1) + part),
        vmem((PARTS, lev - 1, nc - 1) + part),
        vmem((PARTS, lev, nx) + part),
        vmem((PARTS, pairs, nc - 1) + part),
        vmem((PARTS, pairs, nc - 1) + part),
        vmem((PARTS, pairs) + part),
        vmem((lev,) + block, F32),
        dma(2 * pairs),
        dma(2 * lev),
        pltpu.SemaphoreType.DMA,
    ]
    scratch += [pltpu.SemaphoreType.DMA] * 6
    scratch += [dma(pairs)] * 10
    scratch += [dma(PARTS, pairs)] * 2
    scratch += [dma(PARTS, lev - 1)] * 2
    scratch += [dma(PARTS, lev)] * 2
    scratch += [dma(PARTS, pairs)] * 2
    scratch += [dma(lev)] * 2
    anywhere = pl.BlockSpec(memory_space=pl.ANY)
    scalars = pl.BlockSpec(memory_space=pltpu.SMEM)
    result = pl.pallas_call(
        functools.partial(sweep_kernel, (lev, nx, nc, rows, width, PARTS)),
        out_shape=jax.ShapeDtypeStruct((lev, nx, rows, width), F32),
        in_specs=[anywhere, anywhere, scalars, anywhere, scalars, anywhere, anywhere],
        out_specs=anywhere,
        scratch_shapes=scratch,
        compiler_params=pltpu.CompilerParams(
            collective_id=0, has_side_effects=True, vmem_limit_bytes=60 * 1024 * 1024
        ),
    )(
        right_sides, lower_blocks, jnp.transpose(lower_fill, (1, 2, 0)),
        upper_blocks, jnp.transpose(upper_fill, (1, 2, 0)), lower_inv, upper_inv,
    )
    return jnp.transpose(result, (0, 2, 1, 3))


def solution(mesh):
    placed = (
        P(None, "row", "col", None),
        P(None, "col", "row", None, None),
        P(None, "col", "row"),
        P(None, "col", "row", None, None),
        P(None, "col", "row"),
        P(None, "col", None, None),
        P(None, "col", None, None),
    )
    return jax.shard_map(
        per_device,
        mesh=mesh,
        in_specs=placed,
        out_specs=P(None, "row", "col", None),
        check_vma=False,
    )
```

```python
import functools

import jax
import jax.numpy as jnp
from jax import lax
from jax.experimental import pallas as pl
from jax.experimental.pallas import tpu as pltpu
from jax.sharding import PartitionSpec as P

MESH = pl.DeviceIdType.MESH
F32 = jnp.float32
BF16 = jnp.bfloat16
PARTS = 2


def pair_index(current, earlier):
    upper_level = max(current, earlier)
    lower_level = min(current, earlier)
    return upper_level * (upper_level - 1) // 2 + lower_level


def sweep_kernel(
    dims, rhs_raw, lower, lower_fill, upper, upper_fill, lower_inv, upper_inv, out,
    l_raw, u_raw, linv, uinv, l_loc, l_in, l_sum, l_home, u_in, u_sum, u_slice, u_home,
    rhs_home, fwd, flag_out, flag_x, flag_row, flag_all, flags,
    rhs_tile, rhs, raw_sem,
    near, part_out, part_in, solved, pick_out, pick_in, pick_own, answer,
    load_sem, inv_sem, flag_sem,
    rhs_s, rhs_r, fx_s, fx_r, fd_s, fd_r, ly_s, ly_r, ld_s, ld_r, ux_s, ux_r, uz_s, uz_r,
    ua_s, ua_r, na_s, na_r, pb_s, pb_r, xa_s, xa_r, xb_s, xb_r, out_s, out_r,
):
    lev, nx, nc, rows, width, parts = dims
    share = rows * nx // parts
    pairs = lev * (lev - 1) // 2
    nz = nc
    step = width // nc
    row = lax.axis_index("row")
    c = lax.axis_index("col")
    z = lax.div(row, nx)
    x = lax.rem(row, nx)
    diagonal = c == z

    def wrap(value, count):
        return lax.rem(value, count)

    def send(src, dst, ssem, rsem, to_row, to_col):
        pltpu.make_async_remote_copy(
            src_ref=src, dst_ref=dst, send_sem=ssem, recv_sem=rsem,
            device_id=(to_row, to_col), device_id_type=MESH,
        ).start()

    def wait(ref, sem):
        pltpu.make_async_copy(ref, ref, sem).wait()

    def x_peer(k):
        return z * nx + wrap(x + k, nx)

    def z_peer(k):
        return wrap(z + k, nz) * nx + x

    def each(count, body):
        def run(k, carry):
            body(k)
            return carry

        lax.fori_loop(1, count, run, 0)

    order = []
    for a in range(1, lev):
        for b in range(a):
            order.append(pair_index(a, b))
    back = []
    for b in range(lev - 2, -1, -1):
        for a in range(b + 1, lev):
            back.append(pair_index(a, b))

    def load_lower(p):
        return pltpu.make_async_copy(lower.at[p, :, 0], l_raw.at[p], load_sem.at[p])

    def load_upper(p):
        return pltpu.make_async_copy(upper.at[p, :, 0], u_raw.at[p], load_sem.at[pairs + p])

    def load_linv(l):
        return pltpu.make_async_copy(lower_inv.at[l, x], linv.at[l], inv_sem.at[l])

    def load_uinv(l):
        return pltpu.make_async_copy(upper_inv.at[l, x], uinv.at[l], inv_sem.at[lev + l])

    barrier = pltpu.get_barrier_semaphore()

    def greet(to_row, to_col):
        pl.semaphore_signal(barrier, inc=1, device_id=(to_row, to_col), device_id_type=MESH)


    def greet_diagonal(cc):
        @pl.when(jnp.logical_not(jnp.logical_and(diagonal, cc == c)))
        def _():
            greet(c * nx + x, cc)

    def greet_run(k, carry):
        greet_diagonal(k)
        return carry

    lax.fori_loop(0, nc, greet_run, 0)
    each(nz, lambda k: greet(z_peer(k), c))
    each(nc, lambda k: greet(row, wrap(c + k, nc)))
    each(nx, lambda k: greet(x_peer(k), c))

    fetch = pltpu.make_async_copy(rhs_raw, rhs_tile, raw_sem)
    fetch.start()
    load_lower(order[0]).start()
    load_upper(back[0]).start()
    load_linv(0).start()
    load_upper(back[1]).start()
    for p in order[1:]:
        load_lower(p).start()
    for l in range(1, lev):
        load_linv(l).start()
    for p in back[2:]:
        load_upper(p).start()
    for l in range(lev - 1, -1, -1):
        load_uinv(l).start()

    fetch.wait()
    for l in range(lev):
        for t in range(nx):
            rhs[t, l] = rhs_tile[l, :, t, :]

    lane = lax.broadcasted_iota(jnp.int32, (8, 128), 1)
    for t in range(nx):
        tile = jnp.zeros((8, 128), F32)
        for p in range(pairs):
            tile = jnp.where(lane == p, lower_fill[t, 0, p].astype(F32), tile)
            tile = jnp.where(lane == pairs + p, upper_fill[t, 0, p].astype(F32), tile)
        flag_out[t] = tile
    flag_x[x] = flag_out[x]

    pl.semaphore_wait(barrier, (nx - 1) + (nc - 1) + (nz - 1) + nc - diagonal.astype(jnp.int32))

    own_rows = pl.ds(pl.multiple_of(x * rows, rows), rows)

    def start_x(k):
        target = wrap(x + k, nx)
        send(flag_out.at[target], flag_x.at[x], fx_s, fx_r, x_peer(k), c)
        send(rhs.at[target], rhs_home.at[:, own_rows, :], rhs_s, rhs_r, x_peer(k), c)

    each(nx, start_x)
    pltpu.make_async_copy(rhs.at[x], rhs_home.at[:, own_rows, :], rhs_r).start()

    def chunk(index):
        return pl.ds(pl.multiple_of(index * step, step), step)

    def lower_to_columns(p):
        load_lower(p).wait()
        found = jnp.zeros((width, width), BF16)
        for t in range(nx):
            found = lax.select(lower_fill[t, 0, p] != 0, l_raw[p, t], found)
        l_loc[p] = found

        def go(k):
            peer = wrap(c + k, nc)
            send(l_loc.at[p, chunk(peer)], l_in.at[p, k - 1], ly_s.at[p], ly_r.at[p], row, peer)

        each(nc, go)

    def over_z(body):
        def run(zz, carry):
            same = jnp.logical_and(zz == z, diagonal)

            @pl.when(same)
            def _():
                body(zz, True)

            @pl.when(jnp.logical_not(same))
            def _():
                body(zz, False)

            return carry

        lax.fori_loop(0, nz, run, 0)

    def lower_to_home(p):
        wait(l_in.at[p], ly_r.at[p])
        total = l_loc[p, chunk(c), :]
        for k in range(nc - 1):
            total = total + l_in[p, k]
        l_sum[p] = total

        def go(zz, same):
            if same:
                pltpu.make_async_copy(l_sum.at[p], l_home.at[p, chunk(c)], ld_r.at[p]).start()
            else:
                send(
                    l_sum.at[p], l_home.at[p, chunk(c)], ld_s.at[p], ld_r.at[p],
                    zz * nx + x, z,
                )

        over_z(go)

    def flags_to_home():
        wait(flag_x.at[pl.ds(0, nx - 1)], fx_r)
        sub = lax.broadcasted_iota(jnp.int32, (8, 128), 0)
        tile = jnp.zeros((8, 128), F32)
        for k in range(nx):
            tile = jnp.where(sub == k, flag_x[k], tile)
        flag_row[...] = tile

        def go(zz, same):
            if same:
                pltpu.make_async_copy(flag_row, flag_all.at[c], fd_r).start()
            else:
                send(flag_row, flag_all.at[c], fd_s, fd_r, zz * nx + x, z)

        over_z(go)

    def flags_ready():
        wait(flag_all, fd_r)
        copy = pltpu.make_async_copy(flag_all, flags, flag_sem)
        copy.start()
        copy.wait()

    def upper_over_x(p):
        load_upper(p).wait()
        for t in range(nx):
            u_raw[p, t] = lax.select(
                upper_fill[t, 0, p] != 0, u_raw[p, t], jnp.zeros((width, width), BF16)
            )

        def go(k):
            send(u_raw.at[p, wrap(x + k, nx)], u_in.at[p, k - 1], ux_s.at[p], ux_r.at[p], x_peer(k), c)

        each(nx, go)

    def upper_over_z(p):
        wait(u_in.at[p], ux_r.at[p])
        total = u_raw[p, x]
        for k in range(nx - 1):
            total = total + u_in[p, k]
        u_sum[p] = total

        def go(k):
            send(
                u_sum.at[p, chunk(wrap(z + k, nz))], u_slice.at[p, k - 1], uz_s.at[p], uz_r.at[p],
                z_peer(k), c,
            )

        each(nz, go)

    def upper_to_all(p):
        wait(u_slice.at[p], uz_r.at[p])
        total = u_sum[p, chunk(z), :]
        for k in range(nz - 1):
            total = total + u_slice[p, k]
        u_home[p, chunk(z), :] = total

        def go(k):
            send(u_home.at[p, chunk(z)], u_home.at[p, chunk(z)], ua_s.at[p], ua_r.at[p], z_peer(k), c)

        each(nz, go)

    def product(left, right):
        return jnp.dot(left, right, preferred_element_type=F32)

    def over_parts(body):
        def run(h, carry):
            body(h)
            return carry

        lax.fori_loop(0, parts, run, 0)

    def part_rows(h):
        return pl.ds(pl.multiple_of(h * share, share), share)

    def lower_ready(p):
        wait(l_home.at[p], ld_r.at[p])

    def contribute(h, a, b):
        p = pair_index(a, b)
        near[h, p, x] = product(fwd[b, part_rows(h), :], l_home[p]).astype(BF16)

        def go(k):
            send(
                near.at[h, p, x], near.at[h, p, x], na_s.at[h, p], na_r.at[h, p], x_peer(k), c
            )

        each(nx, go)

    def mix(h, column, level):
        total = None
        for m in range(level):
            p = pair_index(level, m)
            for k in range(nx):
                term = near[h, p, k].astype(F32) * flags[column, k, p]
                total = term if total is None else total + term
        return total

    def spread_parts(h, level):
        for m in range(level):
            p = pair_index(level, m)
            wait(near.at[h, p, pl.ds(0, nx - 1)], na_r.at[h, p])

        def go(k):
            peer = wrap(c + k, nc)
            part_out[h, level - 1, k - 1] = mix(h, peer, level).astype(BF16)
            send(
                part_out.at[h, level - 1, k - 1], part_in.at[h, level - 1, k - 1],
                pb_s.at[h, level - 1], pb_r.at[h, level - 1], row, peer,
            )

        each(nc, go)

    def collect_parts(h, level):
        total = mix(h, c, level)
        wait(part_in.at[h, level - 1], pb_r.at[h, level - 1])
        for k in range(nc - 1):
            total = total + part_in[h, level - 1, k].astype(F32)
        return (rhs_home[level, part_rows(h), :].astype(F32) - total).astype(BF16)

    def solve_lower(h, level, residual):
        fwd[level, part_rows(h), :] = product(residual, linv[level]).astype(BF16)

    def solve_upper(h, level, residual):
        result = product(residual, uinv[level])
        if level:
            solved[h, level, x] = result.astype(BF16)

            def go(k):
                send(
                    solved.at[h, level, x], solved.at[h, level, x],
                    xa_s.at[h, level], xa_r.at[h, level], x_peer(k), c,
                )

            each(nx, go)
        answer[level, part_rows(h), :] = result

    def give_answer(level):
        def go(k):
            target = wrap(x + k, nx)
            there = pl.ds(pl.multiple_of(target * rows, rows), rows)
            send(
                answer.at[level, there], out.at[level, x], out_s.at[level], out_r.at[level],
                x_peer(k), c,
            )

        each(nx, go)
        pltpu.make_async_copy(answer.at[level, own_rows], out.at[level, x], out_r.at[level]).start()

    def give_part(h):
        for u in range(nx // parts):
            target = h * (nx // parts) + u
            there = pl.ds(pl.multiple_of(target * rows, rows), rows)

            @pl.when(target == x)
            def _():
                pltpu.make_async_copy(answer.at[0, there], out.at[0, x], out_r.at[0]).start()

            @pl.when(target != x)
            def _():
                send(
                    answer.at[0, there], out.at[0, x], out_s.at[0], out_r.at[0],
                    z * nx + target, c,
                )

    def choose(h, column, a, p):
        total = None
        for k in range(nx):
            term = solved[h, a, k].astype(F32) * flags[column, k, pairs + p]
            total = term if total is None else total + term
        return total.astype(BF16)

    def solved_ready(h, a):
        wait(solved.at[h, a, pl.ds(0, nx - 1)], xa_r.at[h, a])

    def spread_solved(h, a, b):
        p = pair_index(a, b)

        def go(k):
            peer = wrap(c + k, nc)
            pick_out[h, p, k - 1] = choose(h, peer, a, p)
            send(
                pick_out.at[h, p, k - 1], pick_in.at[h, p, k - 1],
                xb_s.at[h, p], xb_r.at[h, p], row, peer,
            )

        each(nc, go)
        pick_own[h, p] = choose(h, c, a, p)

    def upper_ready(p):
        wait(u_home.at[p, pl.ds(0, width - step)], ua_r.at[p])

    def gather_solved(h, a, b):
        p = pair_index(a, b)
        wait(pick_in.at[h, p], xb_r.at[h, p])
        source = pick_own[h, p]
        for k in range(nc - 1):
            source = source + pick_in[h, p, k]
        return product(source, u_home[p])

    def first_level(h):
        solve_lower(h, 0, rhs_home[0, part_rows(h), :])

    def next_level(level):
        load_linv(level).wait()
        lower_ready(pair_index(level + 1, level))

        def body(h):
            solve_lower(h, level, collect_parts(h, level))
            contribute(h, level + 1, level)

        over_parts(body)

    def back_level(level):
        load_uinv(level).wait()
        for a in range(level + 1, lev):
            upper_ready(pair_index(a, level))

        def body(h):
            total = None
            for a in range(lev - 1, level, -1):
                term = gather_solved(h, a, level)
                total = term if total is None else total + term
            residual = (fwd[level, part_rows(h), :].astype(F32) - total).astype(BF16)
            solve_upper(h, level, residual)
            if not level:
                give_part(h)

        over_parts(body)
        if level:
            give_answer(level)

    def turn(h):
        solve_lower(h, 3, collect_parts(h, 3))
        solve_upper(h, 3, fwd[3, part_rows(h), :])

    def pass_up(a, b):
        lower_ready(pair_index(a, b))
        over_parts(lambda h: contribute(h, a, b))

    def pass_down(a, b, arrived=False):
        def body(h):
            if arrived:
                solved_ready(h, a)
            spread_solved(h, a, b)

        over_parts(body)

    idx = pair_index
    lower_to_columns(idx(1, 0))
    upper_over_x(idx(3, 2))
    flags_to_home()
    wait(rhs_home, rhs_r)
    load_linv(0).wait()
    over_parts(first_level)
    lower_to_home(idx(1, 0))
    lower_to_columns(idx(2, 1))
    lower_to_columns(idx(2, 0))
    for b in range(3):
        lower_to_columns(idx(3, b))
    upper_over_x(idx(2, 1))
    lower_to_home(idx(2, 1))
    pass_up(1, 0)
    lower_to_home(idx(2, 0))
    lower_to_home(idx(3, 0))
    flags_ready()
    upper_over_x(idx(3, 1))
    upper_over_z(idx(3, 2))
    over_parts(lambda h: spread_parts(h, 1))
    next_level(1)
    lower_to_home(idx(3, 1))
    lower_to_home(idx(3, 2))
    pass_up(2, 0)
    upper_over_z(idx(2, 1))
    over_parts(lambda h: spread_parts(h, 2))
    upper_over_x(idx(1, 0))
    upper_to_all(idx(3, 2))
    next_level(2)
    pass_up(3, 0)
    pass_up(3, 1)
    upper_over_z(idx(3, 1))
    upper_to_all(idx(2, 1))
    over_parts(lambda h: spread_parts(h, 3))
    upper_over_x(idx(2, 0))
    load_linv(3).wait()
    load_uinv(3).wait()
    over_parts(turn)
    give_answer(3)
    upper_over_z(idx(1, 0))
    upper_to_all(idx(3, 1))
    pass_down(3, 2, True)
    upper_over_x(idx(3, 0))
    pass_down(3, 1)
    upper_over_z(idx(2, 0))
    back_level(2)
    upper_to_all(idx(1, 0))
    pass_down(2, 1, True)
    pass_down(3, 0)
    upper_over_z(idx(3, 0))
    upper_to_all(idx(2, 0))
    back_level(1)
    pass_down(2, 0)
    upper_to_all(idx(3, 0))
    pass_down(1, 0, True)
    back_level(0)

    for p in range(pairs):
        wait(l_in.at[p], ly_s.at[p])
        wait(u_in.at[p], ux_s.at[p])
        wait(u_slice.at[p], uz_s.at[p])
        wait(u_slice.at[p], ua_s.at[p])
        for h in range(parts):
            wait(near.at[h, p, pl.ds(0, nx - 1)], na_s.at[h, p])
            wait(pick_in.at[h, p], xb_s.at[h, p])
    for l in range(lev - 1):
        for h in range(parts):
            wait(part_in.at[h, l], pb_s.at[h, l])
            wait(solved.at[h, l + 1, pl.ds(0, nx - 1)], xa_s.at[h, l + 1])
    wait(flag_x.at[pl.ds(0, nx - 1)], fx_s)
    wait(rhs_home.at[pl.ds(0, nx - 1)] if lev == nx else rhs.at[pl.ds(0, nx - 1)], rhs_s)

    @pl.when(diagonal)
    def _():
        for p in range(pairs):
            wait(l_home.at[p, pl.ds(0, width - step)], ld_s.at[p])
        wait(flag_all.at[pl.ds(0, nz - 1)], fd_s)

    @pl.when(jnp.logical_not(diagonal))
    def _():
        for p in range(pairs):
            wait(l_home.at[p], ld_s.at[p])
        wait(flag_all, fd_s)

    for l in range(lev):
        wait(out.at[l, pl.ds(0, nx - 1)], out_s.at[l])
        wait(out.at[l], out_r.at[l])


def per_device(
    right_sides, lower_blocks, lower_fill, upper_blocks, upper_fill, lower_inv, upper_inv
):
    lev, rows, nx, width = right_sides.shape
    nc = lax.axis_size("col")
    pairs = lev * (lev - 1) // 2
    step = width // nc
    wide = rows * nx

    def vmem(shape, dtype=BF16):
        return pltpu.VMEM(shape, dtype)

    def dma(*shape):
        return pltpu.SemaphoreType.DMA(shape)

    square = (width, width)
    block = (wide, width)
    part = (wide // PARTS, width)
    scratch = [
        vmem((pairs, nx) + square),
        vmem((pairs, nx) + square),
        vmem((lev,) + square),
        vmem((lev,) + square),
        vmem((pairs,) + square),
        vmem((pairs, nc - 1, step, width)),
        vmem((pairs, step, width)),
        vmem((pairs,) + square),
        vmem((pairs, nx - 1) + square),
        vmem((pairs,) + square),
        vmem((pairs, nc - 1, step, width)),
        vmem((pairs,) + square),
        vmem((lev,) + block),
        vmem((lev,) + block),
        vmem((nx, 8, 128), F32),
        vmem((nx, 8, 128), F32),
        vmem((8, 128), F32),
        vmem((nc, 8, 128), F32),
        pltpu.SMEM((nc, 8, 128), F32),
        vmem((lev, rows, nx, width)),
        vmem((nx, lev, rows, width)),
        pltpu.SemaphoreType.DMA,
        vmem((PARTS, pairs, nx) + part),
        vmem((PARTS, lev - 1, nc - 1) + part),
        vmem((PARTS, lev - 1, nc - 1) + part),
        vmem((PARTS, lev, nx) + part),
        vmem((PARTS, pairs, nc - 1) + part),
        vmem((PARTS, pairs, nc - 1) + part),
        vmem((PARTS, pairs) + part),
        vmem((lev,) + block, F32),
        dma(2 * pairs),
        dma(2 * lev),
        pltpu.SemaphoreType.DMA,
    ]
    scratch += [pltpu.SemaphoreType.DMA] * 6
    scratch += [dma(pairs)] * 10
    scratch += [dma(PARTS, pairs)] * 2
    scratch += [dma(PARTS, lev - 1)] * 2
    scratch += [dma(PARTS, lev)] * 2
    scratch += [dma(PARTS, pairs)] * 2
    scratch += [dma(lev)] * 2
    anywhere = pl.BlockSpec(memory_space=pl.ANY)
    scalars = pl.BlockSpec(memory_space=pltpu.SMEM)
    result = pl.pallas_call(
        functools.partial(sweep_kernel, (lev, nx, nc, rows, width, PARTS)),
        out_shape=jax.ShapeDtypeStruct((lev, nx, rows, width), F32),
        in_specs=[anywhere, anywhere, scalars, anywhere, scalars, anywhere, anywhere],
        out_specs=anywhere,
        scratch_shapes=scratch,
        compiler_params=pltpu.CompilerParams(
            collective_id=0, has_side_effects=True, vmem_limit_bytes=60 * 1024 * 1024
        ),
    )(
        right_sides, lower_blocks, jnp.transpose(lower_fill, (1, 2, 0)),
        upper_blocks, jnp.transpose(upper_fill, (1, 2, 0)), lower_inv, upper_inv,
    )
    return jnp.transpose(result, (0, 2, 1, 3))


def solution(mesh):
    placed = (
        P(None, "row", "col", None),
        P(None, "col", "row", None, None),
        P(None, "col", "row"),
        P(None, "col", "row", None, None),
        P(None, "col", "row"),
        P(None, "col", None, None),
        P(None, "col", None, None),
    )
    return jax.shard_map(
        per_device,
        mesh=mesh,
        in_specs=placed,
        out_specs=P(None, "row", "col", None),
        check_vma=False,
    )
```

```python
import functools

import jax
import jax.numpy as jnp
from jax import lax
from jax.experimental import pallas as pl
from jax.experimental.pallas import tpu as pltpu
from jax.sharding import PartitionSpec as P

MESH = pl.DeviceIdType.MESH
F32 = jnp.float32
BF16 = jnp.bfloat16
PARTS = 2


def pair_index(current, earlier):
    upper_level = max(current, earlier)
    lower_level = min(current, earlier)
    return upper_level * (upper_level - 1) // 2 + lower_level


def sweep_kernel(
    dims, rhs_raw, lower, lower_fill, upper, upper_fill, lower_inv, upper_inv, out,
    l_raw, u_raw, linv, uinv, l_loc, l_in, l_sum, l_home, u_in, u_sum, u_slice, u_home,
    rhs_home, fwd, flag_out, flag_x, flag_row, flag_all, flags,
    rhs_tile, rhs, raw_sem,
    near, part_out, part_in, solved, pick_out, pick_in, pick_own, answer,
    load_sem, inv_sem, flag_sem,
    rhs_s, rhs_r, fx_s, fx_r, fd_s, fd_r, ly_s, ly_r, ld_s, ld_r, ux_s, ux_r, uz_s, uz_r,
    ua_s, ua_r, na_s, na_r, pb_s, pb_r, xa_s, xa_r, xb_s, xb_r, out_s, out_r,
):
    lev, nx, nc, rows, width, parts = dims
    share = rows * nx // parts
    pairs = lev * (lev - 1) // 2
    nz = nc
    step = width // nc
    row = lax.axis_index("row")
    c = lax.axis_index("col")
    z = lax.div(row, nx)
    x = lax.rem(row, nx)
    diagonal = c == z

    def wrap(value, count):
        return lax.rem(value, count)

    def send(src, dst, ssem, rsem, to_row, to_col):
        pltpu.make_async_remote_copy(
            src_ref=src, dst_ref=dst, send_sem=ssem, recv_sem=rsem,
            device_id=(to_row, to_col), device_id_type=MESH,
        ).start()

    def wait(ref, sem):
        pltpu.make_async_copy(ref, ref, sem).wait()

    def x_peer(k):
        return z * nx + wrap(x + k, nx)

    def z_peer(k):
        return wrap(z + k, nz) * nx + x

    def each(count, body):
        def run(k, carry):
            body(k)
            return carry

        lax.fori_loop(1, count, run, 0)

    order = []
    for a in range(1, lev):
        for b in range(a):
            order.append(pair_index(a, b))
    back = []
    for b in range(lev - 2, -1, -1):
        for a in range(b + 1, lev):
            back.append(pair_index(a, b))

    def load_lower(p):
        return pltpu.make_async_copy(lower.at[p, :, 0], l_raw.at[p], load_sem.at[p])

    def load_upper(p):
        return pltpu.make_async_copy(upper.at[p, :, 0], u_raw.at[p], load_sem.at[pairs + p])

    def load_linv(l):
        return pltpu.make_async_copy(lower_inv.at[l, x], linv.at[l], inv_sem.at[l])

    def load_uinv(l):
        return pltpu.make_async_copy(upper_inv.at[l, x], uinv.at[l], inv_sem.at[lev + l])

    barrier = pltpu.get_barrier_semaphore()

    def greet(to_row, to_col):
        pl.semaphore_signal(barrier, inc=1, device_id=(to_row, to_col), device_id_type=MESH)


    def greet_diagonal(cc):
        @pl.when(jnp.logical_not(jnp.logical_and(diagonal, cc == c)))
        def _():
            greet(c * nx + x, cc)

    def greet_run(k, carry):
        greet_diagonal(k)
        return carry

    lax.fori_loop(0, nc, greet_run, 0)
    each(nz, lambda k: greet(z_peer(k), c))
    each(nc, lambda k: greet(row, wrap(c + k, nc)))
    each(nx, lambda k: greet(x_peer(k), c))

    fetch = pltpu.make_async_copy(rhs_raw, rhs_tile, raw_sem)
    fetch.start()
    load_lower(order[0]).start()
    load_upper(back[0]).start()
    load_linv(0).start()
    load_upper(back[1]).start()
    for p in order[1:]:
        load_lower(p).start()
    for l in range(1, lev):
        load_linv(l).start()
    for p in back[2:]:
        load_upper(p).start()
    for l in range(lev - 1, -1, -1):
        load_uinv(l).start()

    fetch.wait()
    for l in range(lev):
        for t in range(nx):
            rhs[t, l] = rhs_tile[l, :, t, :]

    lane = lax.broadcasted_iota(jnp.int32, (8, 128), 1)
    for t in range(nx):
        tile = jnp.zeros((8, 128), F32)
        for p in range(pairs):
            tile = jnp.where(lane == p, lower_fill[t, 0, p].astype(F32), tile)
            tile = jnp.where(lane == pairs + p, upper_fill[t, 0, p].astype(F32), tile)
        flag_out[t] = tile
    flag_x[x] = flag_out[x]

    pl.semaphore_wait(barrier, (nx - 1) + (nc - 1) + (nz - 1) + nc - diagonal.astype(jnp.int32))

    own_rows = pl.ds(pl.multiple_of(x * rows, rows), rows)

    def start_x(k):
        target = wrap(x + k, nx)
        send(flag_out.at[target], flag_x.at[x], fx_s, fx_r, x_peer(k), c)
        send(rhs.at[target], rhs_home.at[:, own_rows, :], rhs_s, rhs_r, x_peer(k), c)

    each(nx, start_x)
    pltpu.make_async_copy(rhs.at[x], rhs_home.at[:, own_rows, :], rhs_r).start()

    def chunk(index):
        return pl.ds(pl.multiple_of(index * step, step), step)

    def lower_to_columns(p):
        load_lower(p).wait()
        found = jnp.zeros((width, width), BF16)
        for t in range(nx):
            found = lax.select(lower_fill[t, 0, p] != 0, l_raw[p, t], found)
        l_loc[p] = found

        def go(k):
            peer = wrap(c + k, nc)
            send(l_loc.at[p, chunk(peer)], l_in.at[p, k - 1], ly_s.at[p], ly_r.at[p], row, peer)

        each(nc, go)

    def over_z(body):
        def run(zz, carry):
            same = jnp.logical_and(zz == z, diagonal)

            @pl.when(same)
            def _():
                body(zz, True)

            @pl.when(jnp.logical_not(same))
            def _():
                body(zz, False)

            return carry

        lax.fori_loop(0, nz, run, 0)

    def lower_to_home(p):
        wait(l_in.at[p], ly_r.at[p])
        total = l_loc[p, chunk(c), :]
        for k in range(nc - 1):
            total = total + l_in[p, k]
        l_sum[p] = total

        def go(zz, same):
            if same:
                pltpu.make_async_copy(l_sum.at[p], l_home.at[p, chunk(c)], ld_r.at[p]).start()
            else:
                send(
                    l_sum.at[p], l_home.at[p, chunk(c)], ld_s.at[p], ld_r.at[p],
                    zz * nx + x, z,
                )

        over_z(go)

    def flags_to_home():
        wait(flag_x.at[pl.ds(0, nx - 1)], fx_r)
        sub = lax.broadcasted_iota(jnp.int32, (8, 128), 0)
        tile = jnp.zeros((8, 128), F32)
        for k in range(nx):
            tile = jnp.where(sub == k, flag_x[k], tile)
        flag_row[...] = tile

        def go(zz, same):
            if same:
                pltpu.make_async_copy(flag_row, flag_all.at[c], fd_r).start()
            else:
                send(flag_row, flag_all.at[c], fd_s, fd_r, zz * nx + x, z)

        over_z(go)

    def flags_ready():
        wait(flag_all, fd_r)
        copy = pltpu.make_async_copy(flag_all, flags, flag_sem)
        copy.start()
        copy.wait()

    def upper_over_x(p):
        load_upper(p).wait()
        for t in range(nx):
            u_raw[p, t] = lax.select(
                upper_fill[t, 0, p] != 0, u_raw[p, t], jnp.zeros((width, width), BF16)
            )

        def go(k):
            send(u_raw.at[p, wrap(x + k, nx)], u_in.at[p, k - 1], ux_s.at[p], ux_r.at[p], x_peer(k), c)

        each(nx, go)

    def upper_over_z(p):
        wait(u_in.at[p], ux_r.at[p])
        total = u_raw[p, x]
        for k in range(nx - 1):
            total = total + u_in[p, k]
        u_sum[p] = total

        def go(k):
            send(
                u_sum.at[p, chunk(wrap(z + k, nz))], u_slice.at[p, k - 1], uz_s.at[p], uz_r.at[p],
                z_peer(k), c,
            )

        each(nz, go)

    def upper_to_all(p):
        wait(u_slice.at[p], uz_r.at[p])
        total = u_sum[p, chunk(z), :]
        for k in range(nz - 1):
            total = total + u_slice[p, k]
        u_home[p, chunk(z), :] = total

        def go(k):
            send(u_home.at[p, chunk(z)], u_home.at[p, chunk(z)], ua_s.at[p], ua_r.at[p], z_peer(k), c)

        each(nz, go)

    def product(left, right):
        return jnp.dot(left, right, preferred_element_type=F32)

    def over_parts(body):
        def run(h, carry):
            body(h)
            return carry

        lax.fori_loop(0, parts, run, 0)

    def part_rows(h):
        return pl.ds(pl.multiple_of(h * share, share), share)

    def lower_ready(p):
        wait(l_home.at[p], ld_r.at[p])

    def contribute(h, a, b):
        p = pair_index(a, b)
        near[h, p, x] = product(fwd[b, part_rows(h), :], l_home[p]).astype(BF16)

        def go(k):
            send(
                near.at[h, p, x], near.at[h, p, x], na_s.at[h, p], na_r.at[h, p], x_peer(k), c
            )

        each(nx, go)

    def mix(h, column, level):
        total = None
        for m in range(level):
            p = pair_index(level, m)
            for k in range(nx):
                term = near[h, p, k].astype(F32) * flags[column, k, p]
                total = term if total is None else total + term
        return total

    def spread_parts(h, level):
        for m in range(level):
            p = pair_index(level, m)
            wait(near.at[h, p, pl.ds(0, nx - 1)], na_r.at[h, p])

        def go(k):
            peer = wrap(c + k, nc)
            part_out[h, level - 1, k - 1] = mix(h, peer, level).astype(BF16)
            send(
                part_out.at[h, level - 1, k - 1], part_in.at[h, level - 1, k - 1],
                pb_s.at[h, level - 1], pb_r.at[h, level - 1], row, peer,
            )

        each(nc, go)

    def collect_parts(h, level):
        total = mix(h, c, level)
        wait(part_in.at[h, level - 1], pb_r.at[h, level - 1])
        for k in range(nc - 1):
            total = total + part_in[h, level - 1, k].astype(F32)
        return (rhs_home[level, part_rows(h), :].astype(F32) - total).astype(BF16)

    def solve_lower(h, level, residual):
        fwd[level, part_rows(h), :] = product(residual, linv[level]).astype(BF16)

    def solve_upper(h, level, residual):
        result = product(residual, uinv[level])
        if level:
            solved[h, level, x] = result.astype(BF16)

            def go(k):
                send(
                    solved.at[h, level, x], solved.at[h, level, x],
                    xa_s.at[h, level], xa_r.at[h, level], x_peer(k), c,
                )

            each(nx, go)
        answer[level, part_rows(h), :] = result

    def give_answer(level):
        def go(k):
            target = wrap(x + k, nx)
            there = pl.ds(pl.multiple_of(target * rows, rows), rows)
            send(
                answer.at[level, there], out.at[level, x], out_s.at[level], out_r.at[level],
                x_peer(k), c,
            )

        each(nx, go)
        pltpu.make_async_copy(answer.at[level, own_rows], out.at[level, x], out_r.at[level]).start()

    def give_part(h):
        for u in range(nx // parts):
            target = h * (nx // parts) + u
            there = pl.ds(pl.multiple_of(target * rows, rows), rows)

            @pl.when(target == x)
            def _():
                pltpu.make_async_copy(answer.at[0, there], out.at[0, x], out_r.at[0]).start()

            @pl.when(target != x)
            def _():
                send(
                    answer.at[0, there], out.at[0, x], out_s.at[0], out_r.at[0],
                    z * nx + target, c,
                )

    def choose(h, column, a, p):
        total = None
        for k in range(nx):
            term = solved[h, a, k].astype(F32) * flags[column, k, pairs + p]
            total = term if total is None else total + term
        return total.astype(BF16)

    def solved_ready(h, a):
        wait(solved.at[h, a, pl.ds(0, nx - 1)], xa_r.at[h, a])

    def spread_solved(h, a, b):
        p = pair_index(a, b)

        def go(k):
            peer = wrap(c + k, nc)
            pick_out[h, p, k - 1] = choose(h, peer, a, p)
            send(
                pick_out.at[h, p, k - 1], pick_in.at[h, p, k - 1],
                xb_s.at[h, p], xb_r.at[h, p], row, peer,
            )

        each(nc, go)
        pick_own[h, p] = choose(h, c, a, p)

    def upper_ready(p):
        wait(u_home.at[p, pl.ds(0, width - step)], ua_r.at[p])

    def gather_solved(h, a, b):
        p = pair_index(a, b)
        wait(pick_in.at[h, p], xb_r.at[h, p])
        source = pick_own[h, p]
        for k in range(nc - 1):
            source = source + pick_in[h, p, k]
        return product(source, u_home[p])

    def first_level(h):
        solve_lower(h, 0, rhs_home[0, part_rows(h), :])

    def next_level(level):
        load_linv(level).wait()
        lower_ready(pair_index(level + 1, level))

        def body(h):
            solve_lower(h, level, collect_parts(h, level))
            contribute(h, level + 1, level)

        over_parts(body)

    def back_level(level):
        load_uinv(level).wait()
        for a in range(level + 1, lev):
            upper_ready(pair_index(a, level))

        def body(h):
            total = None
            for a in range(lev - 1, level, -1):
                term = gather_solved(h, a, level)
                total = term if total is None else total + term
            residual = (fwd[level, part_rows(h), :].astype(F32) - total).astype(BF16)
            solve_upper(h, level, residual)
            if not level:
                give_part(h)

        over_parts(body)
        if level:
            give_answer(level)

    def turn(h):
        solve_lower(h, 3, collect_parts(h, 3))
        solve_upper(h, 3, fwd[3, part_rows(h), :])

    def pass_up(a, b):
        lower_ready(pair_index(a, b))
        over_parts(lambda h: contribute(h, a, b))

    def pass_down(a, b, arrived=False):
        def body(h):
            if arrived:
                solved_ready(h, a)
            spread_solved(h, a, b)

        over_parts(body)

    idx = pair_index
    lower_to_columns(idx(1, 0))
    upper_over_x(idx(3, 2))
    flags_to_home()
    wait(rhs_home, rhs_r)
    load_linv(0).wait()
    over_parts(first_level)
    lower_to_home(idx(1, 0))
    lower_to_columns(idx(2, 1))
    lower_to_columns(idx(2, 0))
    for b in range(3):
        lower_to_columns(idx(3, b))
    upper_over_x(idx(2, 1))
    lower_to_home(idx(2, 1))
    pass_up(1, 0)
    lower_to_home(idx(2, 0))
    lower_to_home(idx(3, 0))
    flags_ready()
    upper_over_x(idx(3, 1))
    upper_over_z(idx(3, 2))
    over_parts(lambda h: spread_parts(h, 1))
    next_level(1)
    pass_up(2, 0)
    lower_to_home(idx(3, 2))
    lower_to_home(idx(3, 1))
    upper_over_z(idx(2, 1))
    over_parts(lambda h: spread_parts(h, 2))
    upper_over_x(idx(1, 0))
    upper_to_all(idx(3, 2))
    next_level(2)
    pass_up(3, 0)
    pass_up(3, 1)
    upper_over_z(idx(3, 1))
    upper_to_all(idx(2, 1))
    over_parts(lambda h: spread_parts(h, 3))
    upper_over_x(idx(2, 0))
    load_linv(3).wait()
    load_uinv(3).wait()
    over_parts(turn)
    give_answer(3)
    upper_over_z(idx(1, 0))
    upper_to_all(idx(3, 1))
    pass_down(3, 2, True)
    upper_over_x(idx(3, 0))
    pass_down(3, 1)
    upper_over_z(idx(2, 0))
    back_level(2)
    upper_to_all(idx(1, 0))
    pass_down(2, 1, True)
    pass_down(3, 0)
    upper_over_z(idx(3, 0))
    upper_to_all(idx(2, 0))
    back_level(1)
    pass_down(2, 0)
    upper_to_all(idx(3, 0))
    pass_down(1, 0, True)
    back_level(0)

    for p in range(pairs):
        wait(l_in.at[p], ly_s.at[p])
        wait(u_in.at[p], ux_s.at[p])
        wait(u_slice.at[p], uz_s.at[p])
        wait(u_slice.at[p], ua_s.at[p])
        for h in range(parts):
            wait(near.at[h, p, pl.ds(0, nx - 1)], na_s.at[h, p])
            wait(pick_in.at[h, p], xb_s.at[h, p])
    for l in range(lev - 1):
        for h in range(parts):
            wait(part_in.at[h, l], pb_s.at[h, l])
            wait(solved.at[h, l + 1, pl.ds(0, nx - 1)], xa_s.at[h, l + 1])
    wait(flag_x.at[pl.ds(0, nx - 1)], fx_s)
    wait(rhs_home.at[pl.ds(0, nx - 1)] if lev == nx else rhs.at[pl.ds(0, nx - 1)], rhs_s)

    @pl.when(diagonal)
    def _():
        for p in range(pairs):
            wait(l_home.at[p, pl.ds(0, width - step)], ld_s.at[p])
        wait(flag_all.at[pl.ds(0, nz - 1)], fd_s)

    @pl.when(jnp.logical_not(diagonal))
    def _():
        for p in range(pairs):
            wait(l_home.at[p], ld_s.at[p])
        wait(flag_all, fd_s)

    for l in range(lev):
        wait(out.at[l, pl.ds(0, nx - 1)], out_s.at[l])
        wait(out.at[l], out_r.at[l])


def per_device(
    right_sides, lower_blocks, lower_fill, upper_blocks, upper_fill, lower_inv, upper_inv
):
    lev, rows, nx, width = right_sides.shape
    nc = lax.axis_size("col")
    pairs = lev * (lev - 1) // 2
    step = width // nc
    wide = rows * nx

    def vmem(shape, dtype=BF16):
        return pltpu.VMEM(shape, dtype)

    def dma(*shape):
        return pltpu.SemaphoreType.DMA(shape)

    square = (width, width)
    block = (wide, width)
    part = (wide // PARTS, width)
    scratch = [
        vmem((pairs, nx) + square),
        vmem((pairs, nx) + square),
        vmem((lev,) + square),
        vmem((lev,) + square),
        vmem((pairs,) + square),
        vmem((pairs, nc - 1, step, width)),
        vmem((pairs, step, width)),
        vmem((pairs,) + square),
        vmem((pairs, nx - 1) + square),
        vmem((pairs,) + square),
        vmem((pairs, nc - 1, step, width)),
        vmem((pairs,) + square),
        vmem((lev,) + block),
        vmem((lev,) + block),
        vmem((nx, 8, 128), F32),
        vmem((nx, 8, 128), F32),
        vmem((8, 128), F32),
        vmem((nc, 8, 128), F32),
        pltpu.SMEM((nc, 8, 128), F32),
        vmem((lev, rows, nx, width)),
        vmem((nx, lev, rows, width)),
        pltpu.SemaphoreType.DMA,
        vmem((PARTS, pairs, nx) + part),
        vmem((PARTS, lev - 1, nc - 1) + part),
        vmem((PARTS, lev - 1, nc - 1) + part),
        vmem((PARTS, lev, nx) + part),
        vmem((PARTS, pairs, nc - 1) + part),
        vmem((PARTS, pairs, nc - 1) + part),
        vmem((PARTS, pairs) + part),
        vmem((lev,) + block, F32),
        dma(2 * pairs),
        dma(2 * lev),
        pltpu.SemaphoreType.DMA,
    ]
    scratch += [pltpu.SemaphoreType.DMA] * 6
    scratch += [dma(pairs)] * 10
    scratch += [dma(PARTS, pairs)] * 2
    scratch += [dma(PARTS, lev - 1)] * 2
    scratch += [dma(PARTS, lev)] * 2
    scratch += [dma(PARTS, pairs)] * 2
    scratch += [dma(lev)] * 2
    anywhere = pl.BlockSpec(memory_space=pl.ANY)
    scalars = pl.BlockSpec(memory_space=pltpu.SMEM)
    result = pl.pallas_call(
        functools.partial(sweep_kernel, (lev, nx, nc, rows, width, PARTS)),
        out_shape=jax.ShapeDtypeStruct((lev, nx, rows, width), F32),
        in_specs=[anywhere, anywhere, scalars, anywhere, scalars, anywhere, anywhere],
        out_specs=anywhere,
        scratch_shapes=scratch,
        compiler_params=pltpu.CompilerParams(
            collective_id=0, has_side_effects=True, vmem_limit_bytes=60 * 1024 * 1024
        ),
    )(
        right_sides, lower_blocks, jnp.transpose(lower_fill, (1, 2, 0)),
        upper_blocks, jnp.transpose(upper_fill, (1, 2, 0)), lower_inv, upper_inv,
    )
    return jnp.transpose(result, (0, 2, 1, 3))


def solution(mesh):
    placed = (
        P(None, "row", "col", None),
        P(None, "col", "row", None, None),
        P(None, "col", "row"),
        P(None, "col", "row", None, None),
        P(None, "col", "row"),
        P(None, "col", None, None),
        P(None, "col", None, None),
    )
    return jax.shard_map(
        per_device,
        mesh=mesh,
        in_specs=placed,
        out_specs=P(None, "row", "col", None),
        check_vma=False,
    )
```
